256 devices in a mesh: tm: 32 (over z, x), space: 8 (over y, core).
Axes of the slice: x: 4, y: 4, z: 8, core: 2. Of those that a mesh axis runs over, the one named last changes fastest.
Arguments:
- frames: bfloat16 [128, 32, 128, 128], P('tm', 'space'), may hold values from -6 to 6
- conv_weight: bfloat16 [3456, 128], replicated, may hold values from -0.109375 to 0.109375
- conv_bias: float32 [128], replicated, may hold values from -3 to 3
- projection: float32 [128, 6], replicated, may hold values from -1 to 1
- levels: int32 [6], replicated, may hold values from 3 to 8, as said below
- centres: int32 [32, 32, 768], P(None, 'space', 'tm'), may hold values from 0 to 7, as said below
- code_grad: float32 [32, 32, 768], P(None, 'space', 'tm'), may hold values from -6 to 6
Outputs:
- quantized: float32 [32, 32, 768], P(None, 'space', 'tm')
- weight_grad: float32 [3456, 128], P('tm', 'space')
- projection_grad: float32 [128, 6], replicated
- bias_grad: float32 [128], replicated
The draws below stay inside these ranges and needn't reach their ends.
Inputs may be any that keep to these rules, and one draw needn't show every extreme that they name: Level counts of the FSQ channels; in every draw some channel has 3 levels and some has 8. centres[g, h, q] is below levels[q % 6].
All inputs are finite; a program needn't handle non-finite values.
Results may differ from the reference program's by a relative error of at most 0.0024.
Values may be sent and summed in bfloat16 or wider, within the bound.
No kernel may reach another device: no remote copies, remote signals or barrier semaphores. Data moves between devices by JAX's collectives and lax.ppermute only.
A program may use at most 64 MiB of HBM per device.

```python
import jax
import jax.numpy as jnp
from jax import lax

CH = 128
L = 6
W = 128
F = 128
H = 32
TL = 32
LW = 768
KC = 3456


def level_table(key):
    drawn_base = jax.random.randint(jax.random.fold_in(key, 11), (L,), 3, 9)
    channel_order = jax.random.permutation(jax.random.fold_in(key, 12), L)
    return drawn_base.at[channel_order[0]].set(8).at[channel_order[1]].set(3).astype(jnp.int32)


def draw_levels(key, part):
    return level_table(key)


def draw_centres(key, part):
    column_levels = jnp.tile(level_table(key), W)
    return jax.random.randint(jax.random.fold_in(key, 13), (TL, H, LW), 0, column_levels).astype(jnp.int32)


def level_of(own_key, shape, pieces, smallest, top_value):
    level, own = 1.0, jax.random.fold_in(own_key, 6)
    for position, parts in pieces:
        heights = jnp.exp(jax.random.uniform(jax.random.fold_in(own, position), (parts,), jnp.float32, smallest / len(pieces), top_value / len(pieces)))
        level = level * jnp.repeat(heights, shape[position] // parts).reshape([-1 if axis == position else 1 for axis in range(len(shape))])
    return level


def centred(key, dims, spread, bound, pieces=(), kind=jnp.bfloat16):
    entries = jax.random.normal(key, dims, jnp.float32) * spread
    if len(pieces) > 0:
        entries = level_of(key, dims, pieces, -0.22, 0.18) * entries
    return jnp.clip(entries, min=-bound, max=bound).astype(kind)


def setup_inputs(seed: int = 0) -> dict:
    key_list = jax.random.split(jax.random.key(seed), 8)
    frames = centred(key_list[0], (F, H, W, CH), 1.0, 6.0, ((0, 32), (1, 8)))
    conv_weight = centred(key_list[1], (KC, CH), KC ** -0.5, 0.109375)
    conv_bias = centred(key_list[2], (CH,), 0.5, 3.0, (), jnp.float32)
    projection = centred(key_list[3], (CH, L), (CH // 4) ** -0.5, 1.0, (), jnp.float32)
    levels = draw_levels(jax.random.fold_in(key_list[7], 71), 0)
    centres = draw_centres(jax.random.fold_in(key_list[7], 71), 0)
    code_grad = centred(key_list[6], (TL, H, LW), 1.0, 6.0, ((1, 8), (2, 32)), jnp.float32)
    return {"frames": frames, "conv_weight": conv_weight, "conv_bias": conv_bias, "projection": projection, "levels": levels, "centres": centres, "code_grad": code_grad}


offset_scale = 0.45
commit_weight = 0.25
highest = lax.Precision.HIGHEST


def widen_frames(frame_block):
    frame_width = frame_block.shape[2]
    padded = jnp.pad(frame_block, ((0, 0), (1, 1), (1, 1), (0, 0)))
    return jnp.concatenate([padded[:, :, column_shift:column_shift + frame_width] for column_shift in range(3)], axis=3)


def tap_slabs(widened, frame_count, row_count):
    triple = widened.shape[3]
    slabs = []
    for time_tap in range(3):
        for row_tap in range(3):
            slabs.append(widened[time_tap:time_tap + frame_count, row_tap:row_tap + row_count].reshape(-1, triple))
    return slabs


def reference(frames, conv_weight, conv_bias, projection, levels, centres, code_grad):
    channels = frames.shape[3]
    triple = 3 * channels
    cell_count = H * W
    padded_time = jnp.concatenate([frames[:1], frames[:1], frames], 0)

    def forward(group):
        frame_block = lax.dynamic_slice_in_dim(padded_time, (group * 4).astype(jnp.int32), 6, 0)
        slabs = tap_slabs(widen_frames(frame_block), 4, H)
        preact = jnp.zeros((4 * cell_count, channels), jnp.float32) + conv_bias
        for tap_number in range(9):
            preact = preact + jnp.dot(slabs[tap_number], conv_weight[tap_number * triple:(tap_number + 1) * triple], preferred_element_type=jnp.float32)
        activated = lax.optimization_barrier(jax.nn.silu(preact).astype(jnp.bfloat16))
        pooled = activated.astype(jnp.float32).reshape(4, cell_count, channels).sum(0) * 0.25
        return preact, pooled

    group_index = jnp.arange(TL, dtype=jnp.int32)
    preact_all, pooled_all = lax.map(forward, group_index)
    latent = jnp.dot(pooled_all, projection, precision=highest).reshape(TL, H, LW)
    half_range = (levels.astype(jnp.float32) - 1.0) * 0.5
    half_column = jnp.tile(half_range, W)
    quantized = (centres.astype(jnp.float32) - half_column) / half_column
    squashed = jnp.tanh(latent)
    grad_scale = float(F * H * W) ** -0.5
    code_step = (code_grad / half_column + 2.0 * commit_weight * offset_scale * squashed) * offset_scale * (1.0 - squashed * squashed) * grad_scale
    code_step = code_step.reshape(TL, cell_count, L)
    projection_grad = jnp.einsum("gnc,gnl->cl", pooled_all, code_step, precision=highest)
    pooled_grad = jnp.dot(code_step, projection.T, precision=highest)

    def backward(carry, inputs):
        weight_sum, bias_sum = carry
        preact, grad_group, group = inputs
        frame_block = lax.dynamic_slice_in_dim(padded_time, (group * 4).astype(jnp.int32), 6, 0)
        slabs = tap_slabs(widen_frames(frame_block), 4, H)
        sigmoid_pre = jax.nn.sigmoid(preact)
        silu_slope = sigmoid_pre * (1.0 + preact * (1.0 - sigmoid_pre))
        pre_grad = (0.25 * grad_group[None] * silu_slope.reshape(4, cell_count, channels)).reshape(-1, channels)
        low_grad = pre_grad.astype(jnp.bfloat16)
        blocks = jnp.concatenate([lax.dot_general(tap_slab, low_grad, (((0,), (0,)), ((), ())), preferred_element_type=jnp.float32) for tap_slab in slabs], 0)
        return (weight_sum + blocks, bias_sum + pre_grad.sum(0)), None

    start = (jnp.zeros((27 * channels, channels), jnp.float32), jnp.zeros((channels,), jnp.float32))
    final_carry, unused_out = lax.scan(backward, start, (preact_all, pooled_grad, group_index))
    weight_grad, bias_grad = final_carry
    return quantized, weight_grad, projection_grad, bias_grad
```

```python
import jax
import jax.numpy as jnp
from jax import lax
from jax.experimental import pallas as pl
from jax.experimental.pallas import tpu as pltpu
from jax.sharding import PartitionSpec as P

offset_scale = 0.45
commit_weight = 0.25
highest = lax.Precision.HIGHEST
bf16 = jnp.bfloat16
f32 = jnp.float32
VMEM_BYTES = 48 * 1024 * 1024
CH = 128
L = 6
W = 128
TAPS = 27
LANES = TAPS * CH
WIDE = LANES + CH


def vmem(count):
    return [pl.BlockSpec(memory_space=pltpu.VMEM)] * count


def call(kernel, out_shape, in_specs, scratch=()):
    outs = len(out_shape)
    return pl.pallas_call(
        kernel,
        out_shape=out_shape,
        in_specs=in_specs,
        out_specs=vmem(outs),
        scratch_shapes=list(scratch),
        compiler_params=pltpu.CompilerParams(vmem_limit_bytes=VMEM_BYTES),
    )


def half_ranges(levels_ref, channel):
    half = jnp.ones(channel.shape, f32)
    for j in range(L):
        half = jnp.where(channel == j, (levels_ref[j].astype(f32) - 1.0) * 0.5, half)
    return half


def code_kernel(levels_ref, centres_ref, grad_ref, quantized_ref, out_ref):
    rows, columns, frames = grad_ref.shape
    channel = lax.broadcasted_iota(jnp.int32, (columns, frames), 0) % L
    half = half_ranges(levels_ref, channel)
    parts = []
    for h in range(rows):
        quantized_ref[h] = (centres_ref[h].astype(f32) - half) / half
        parts.append(grad_ref[h] / half)
    stacked = jnp.concatenate(parts, 0)
    padded = jnp.pad(stacked, ((0, CH - rows * columns), (0, CH - frames)))
    turned = padded.T
    out_ref[...] = turned[:frames]


def shifted_rows(value, step):
    row = lax.broadcasted_iota(jnp.int32, value.shape, 0)
    rolled = pltpu.roll(value, step % value.shape[0], 0)
    edge = 0 if step == 1 else value.shape[0] - 1
    return jnp.where(row == edge, 0.0, rolled)


def shifted_lanes(value, step):
    lane = lax.broadcasted_iota(jnp.int32, value.shape, 1)
    rolled = pltpu.roll(value, step % value.shape[1], 1)
    edge = 0 if step == 1 else value.shape[1] - 1
    return jnp.where(lane == edge, 0.0, rolled)


def block_kernel(
    total_cells,
    frames_ref,
    earlier_ref,
    up_ref,
    down_ref,
    corner_up_ref,
    corner_down_ref,
    weight_ref,
    bias_ref,
    projection_ref,
    code_ref,
    mine_ref,
    theirs_ref,
    x_ref,
    wide_ref,
    slope_ref,
    low_ref,
    grad_ref,
):
    first = lax.axis_index("tm") == 0
    space = lax.axis_index("space")
    core = lax.rem(space, 2)
    row_chip = lax.div(space, 2)
    for t in range(4):
        x_ref[t + 2, 0] = up_ref[t]
        x_ref[t + 2, 5] = down_ref[t]
        for h in range(4):
            x_ref[t + 2, h + 1] = frames_ref[t, h]

    @pl.when(first)
    def _():
        for t in range(2):
            x_ref[t, 0] = up_ref[0]
            x_ref[t, 5] = down_ref[0]
            for h in range(4):
                x_ref[t, h + 1] = frames_ref[0, h]

    @pl.when(jnp.logical_not(first))
    def _():
        for t in range(2):
            x_ref[t, 0] = corner_up_ref[t]
            x_ref[t, 5] = corner_down_ref[t]
            for h in range(4):
                x_ref[t, h + 1] = earlier_ref[t, h]

    for tap in range(9):
        for c in range(3):
            wide_ref[tap * CH : (tap + 1) * CH, c * CH : (c + 1) * CH] = weight_ref[
                (3 * tap + c) * CH : (3 * tap + c + 1) * CH, :
            ]
    bias = bias_ref[...]
    pooled = [jnp.zeros((W, CH), f32) for _ in range(4)]
    for t in range(4):
        for h in range(4):
            left = jnp.concatenate([x_ref[t + a, h + b] for a in range(3) for b in range(3)], 1)
            z = jnp.dot(left, wide_ref[...], preferred_element_type=f32)
            preact = (
                bias
                + shifted_rows(z[:, :CH], 1)
                + z[:, CH : 2 * CH]
                + shifted_rows(z[:, 2 * CH :], -1)
            )
            sigmoid = 1.0 / (1.0 + jnp.exp(-preact))
            slope_ref[t, h] = sigmoid * (1.0 + preact * (1.0 - sigmoid))
            pooled[h] = pooled[h] + (preact * sigmoid).astype(bf16).astype(f32)
    pooled = jnp.concatenate(pooled, 0) * 0.25
    projection = jnp.concatenate([projection_ref[...], jnp.zeros((2, CH), f32)], 0)
    latent = lax.dot_general(
        projection, pooled, (((1,), (1,)), ((), ())), precision=highest, preferred_element_type=f32
    )
    squashed = jnp.tanh(latent)
    tile_of = lax.broadcasted_iota(jnp.int32, (W, 32), 1)
    column = lax.broadcasted_iota(jnp.int32, (W, 32), 0)
    spread = jnp.where(column // 4 == tile_of, 1.0, 0.0).astype(f32)
    repeated = jnp.dot(spread, code_ref[...], precision=highest, preferred_element_type=f32)
    place = lax.broadcasted_iota(jnp.int32, (W, CH), 1)
    column = lax.broadcasted_iota(jnp.int32, (W, CH), 0)
    repeated = jnp.where((place % 24) // L == column % 4, repeated, 0.0)
    wanted = lax.broadcasted_iota(jnp.int32, (32, CH), 0)
    place = lax.broadcasted_iota(jnp.int32, (32, CH), 1)
    pick = jnp.where((place // 24 == wanted // 8) & (place % L == wanted % 8), 1.0, 0.0).astype(f32)
    codes = lax.dot_general(
        pick, repeated, (((1,), (1,)), ((), ())), precision=highest, preferred_element_type=f32
    )
    codes = jnp.concatenate([codes[8 * h : 8 * h + 8] for h in range(4)], 1)
    code_step = (
        (codes + 2.0 * commit_weight * offset_scale * squashed)
        * offset_scale
        * (1.0 - squashed * squashed)
        * float(total_cells) ** (-0.5)
    )
    projection_part = jnp.dot(code_step, pooled, precision=highest, preferred_element_type=f32)
    pooled_grad = 0.25 * lax.dot_general(
        code_step, projection, (((0,), (0,)), ((), ())), precision=highest, preferred_element_type=f32
    )
    bias_part = jnp.zeros((8, CH), f32)
    for t in range(4):
        for h in range(4):
            pre_grad = pooled_grad[h * W : (h + 1) * W] * slope_ref[t, h]
            bias_part = bias_part + pre_grad.reshape(W // 8, 8, CH).sum(0)
            turned = pre_grad.T
            place = (t * 4 + h) * W
            low_ref[0:CH, place : place + W] = shifted_lanes(turned, -1).astype(bf16)
            low_ref[CH : 2 * CH, place : place + W] = turned.astype(bf16)
            low_ref[2 * CH :, place : place + W] = shifted_lanes(turned, 1).astype(bf16)
    bias_row = bias_part.sum(0, keepdims=True)
    row = lax.broadcasted_iota(jnp.int32, (8, CH), 0)
    small = jnp.where(row == L, bias_row, projection_part)
    taps = [(a, b) for a in range(3) for b in range(3)]
    for start in range(0, 9, 2):
        group = taps[start : start + 2]
        right = jnp.concatenate(
            [x_ref[a : a + 4, b : b + 4].reshape(16 * W, CH) for a, b in group], 1
        )
        grad_ref[:, start * CH : (start + len(group)) * CH] = jnp.dot(
            low_ref[...], right, preferred_element_type=f32
        )
    for d in range(4):
        target = 32 * (row_chip ^ d)
        for c in range(3):
            own = pl.multiple_of(c * CH + target + 16 * core, 16)
            other = pl.multiple_of(c * CH + target + 16 * (1 - core), 16)
            for tap in range(9):
                to = slice((3 * tap + c) * CH, (3 * tap + c + 1) * CH)
                mine_ref[d, :, to] = grad_ref[pl.ds(own, 16), tap * CH : (tap + 1) * CH]
                theirs_ref[d, :, to] = grad_ref[pl.ds(other, 16), tap * CH : (tap + 1) * CH]
        mine_ref[d, 0:8, LANES:] = small
        mine_ref[d, 8:16, LANES:] = jnp.zeros((8, CH), f32)
        theirs_ref[d, 0:8, LANES:] = small
        theirs_ref[d, 8:16, LANES:] = jnp.zeros((8, CH), f32)


def pair_kernel(mine_ref, got_ref, *outs):
    for d in range(4):
        outs[d][...] = mine_ref[d] + got_ref[d]


def row_kernel(shards, o0_ref, o1_ref, o2_ref, o3_ref, out_ref):
    total = (o0_ref[...] + o1_ref[...]) + (o2_ref[...] + o3_ref[...])
    share = LANES // shards
    small = total[0:8, LANES:]
    for k in range(shards):
        start = k * share
        base = start // CH * CH
        window = total[:, base : base + 2 * CH]
        if start > base:
            window = pltpu.roll(window, 2 * CH - (start - base), 1)
        out_ref[k, 0:16] = window[:, :CH]
        out_ref[k, 16:24] = small


def final_kernel(parts_ref, weight_ref, projection_ref, bias_ref):
    total = parts_ref[0]
    for k in range(1, parts_ref.shape[0]):
        total = total + parts_ref[k]
    weight_ref[...] = total[0:16, : weight_ref.shape[1]]
    projection_ref[...] = total[16 : 16 + L]
    bias_ref[...] = total[16 + L : 17 + L]


def on_device(frames, conv_weight, conv_bias, projection, levels, centres, code_grad):
    shards = lax.axis_size("tm")
    strips = lax.axis_size("space")
    both = ("tm", "space")
    shape = jax.ShapeDtypeStruct
    smem = pl.BlockSpec(memory_space=pltpu.SMEM)

    later = [(i, i + 1) for i in range(shards - 1)]
    lower = [(i, i + 1) for i in range(strips - 1)]
    upper = [(b, a) for a, b in lower]
    later_lower = [(a * strips + p, b * strips + q) for a, b in later for p, q in lower]
    later_upper = [(a * strips + p, b * strips + q) for a, b in later for p, q in upper]
    top, bottom = frames[:, 0], frames[:, 3]
    earlier = lax.ppermute(frames[2:], "tm", later)
    up = lax.ppermute(bottom, "space", lower)
    down = lax.ppermute(top, "space", upper)
    corner_up = lax.ppermute(bottom[2:], both, later_lower)
    corner_down = lax.ppermute(top[2:], both, later_upper)

    code_shape = (code_grad.shape[1], code_grad.shape[2], code_grad.shape[0])
    quantized, codes = call(
        code_kernel,
        [shape(code_shape, f32), shape((shards, CH), f32)],
        [smem] + vmem(2),
    )(levels, jnp.transpose(centres, (1, 2, 0)), jnp.transpose(code_grad, (1, 2, 0)))
    quantized = jnp.transpose(quantized, (2, 0, 1))
    codes = lax.all_to_all(codes.reshape(shards, 1, CH), "tm", 0, 0, tiled=True)
    codes = codes.reshape(shards, CH)

    total_cells = 4 * shards * 4 * strips * W
    mine, theirs = call(
        lambda *refs: block_kernel(total_cells, *refs),
        [shape((4, 16, WIDE), f32)] * 2,
        vmem(10),
        [
            pltpu.VMEM((6, 6, W, CH), bf16),
            pltpu.VMEM((9 * CH, 3 * CH), bf16),
            pltpu.VMEM((4, 4, W, CH), f32),
            pltpu.VMEM((3 * CH, 16 * W), bf16),
            pltpu.VMEM((3 * CH, 9 * CH), f32),
        ],
    )(
        frames,
        earlier,
        up,
        down,
        corner_up,
        corner_down,
        conv_weight,
        conv_bias.reshape(1, CH),
        projection.T,
        codes,
    )

    def swapped(value, step):
        return lax.ppermute(value, "space", [(i, i ^ step) for i in range(strips)])

    summed = call(pair_kernel, [shape((16, WIDE), f32)] * 4, vmem(2))(mine, swapped(theirs, 1))
    received = [summed[0]] + [swapped(summed[d], 2 * d) for d in range(1, 4)]
    (chunks,) = call(
        lambda *refs: row_kernel(shards, *refs), [shape((shards, 24, CH), f32)], vmem(4)
    )(*received)
    parts = lax.all_to_all(chunks, "tm", 0, 0, tiled=True)
    weight_grad, projection_grad, bias_grad = call(
        final_kernel,
        [shape((16, LANES // shards), f32), shape((L, CH), f32), shape((1, CH), f32)],
        vmem(1),
    )(parts)
    return quantized, weight_grad.T, projection_grad.T, bias_grad.reshape(CH)


def solution(mesh):
    return jax.shard_map(
        on_device,
        mesh=mesh,
        in_specs=(
            P("tm", "space", None, None),
            P(),
            P(),
            P(),
            P(),
            P(None, "space", "tm"),
            P(None, "space", "tm"),
        ),
        out_specs=(P(None, "space", "tm"), P("tm", "space"), P(), P()),
        check_vma=False,
    )
```

```python
import jax
import jax.numpy as jnp
from jax import lax
from jax.experimental import pallas as pl
from jax.experimental.pallas import tpu as pltpu
from jax.sharding import PartitionSpec as P

offset_scale = 0.45
commit_weight = 0.25
highest = lax.Precision.HIGHEST
bf16 = jnp.bfloat16
f32 = jnp.float32
MIB = 1024 * 1024
CH = 128
L = 6
W = 128
TAPS = 27
LANES = TAPS * CH
WIDE = LANES + CH
STATE = 16 * W
SMALL = 20 * W


VMEM = pl.BlockSpec(memory_space=pltpu.VMEM)
ANY = pl.BlockSpec(memory_space=pl.ANY)


def call(kernel, out_shape, in_specs, scratch=(), aliases=None):
    return pl.pallas_call(
        kernel,
        out_shape=out_shape,
        in_specs=in_specs,
        out_specs=[VMEM] * len(out_shape),
        scratch_shapes=list(scratch),
        input_output_aliases=aliases or {},
        compiler_params=pltpu.CompilerParams(vmem_limit_bytes=24 * MIB),
    )


def copy_all(pairs, sems):
    copies = [pltpu.make_async_copy(src, dst, sems.at[i]) for i, (src, dst) in enumerate(pairs)]
    for copy in copies:
        copy.start()
    for copy in copies:
        copy.wait()


def half_ranges(levels_ref, channel):
    half = jnp.ones(channel.shape, f32)
    for j in range(L):
        half = jnp.where(channel == j, (levels_ref[j].astype(f32) - 1.0) * 0.5, half)
    return half


def code_kernel(grad_ref, codes_ref):
    rows, columns, frames = grad_ref.shape
    stacked = jnp.concatenate([grad_ref[h] for h in range(rows)], 0)
    padded = jnp.pad(stacked, ((0, CH - rows * columns), (0, CH - frames)))
    codes_ref[...] = padded.T[:frames]


def edge_kernel(frames_any, x_ref, top_ref, bottom_ref, sems):
    copy_all(
        [
            (frames_any, x_ref.at[:, 1:5]),
            (frames_any.at[:, 0], top_ref),
            (frames_any.at[:, 3], bottom_ref),
        ],
        sems,
    )


def late_kernel(own_ref, up_ref, down_ref, x_ref, late_ref):
    for t in range(4):
        x_ref[t, 0] = up_ref[t]
        x_ref[t, 5] = down_ref[t]
    for t in range(2):
        late_ref[t, 0] = up_ref[t + 2]
        late_ref[t, 5] = down_ref[t + 2]
        for h in range(1, 5):
            late_ref[t, h] = own_ref[t + 2, h]


def block_of(early_ref, x_ref):
    return lambda t, h: early_ref[t, h] if t < 2 else x_ref[t - 2, h]


def shifted_rows(value, step):
    row = lax.broadcasted_iota(jnp.int32, value.shape, 0)
    rolled = pltpu.roll(value, step % value.shape[0], 0)
    edge = 0 if step == 1 else value.shape[0] - 1
    return jnp.where(row == edge, 0.0, rolled)


def shifted_lanes(value, step):
    lane = lax.broadcasted_iota(jnp.int32, value.shape, 1)
    rolled = pltpu.roll(value, step % value.shape[1], 1)
    edge = 0 if step == 1 else value.shape[1] - 1
    return jnp.where(lane == edge, 0.0, rolled)


def forward_kernel(
    levels_any,
    centres_any,
    earlier_ref,
    x_ref,
    weight_any,
    bias_any,
    projection_any,
    early_ref,
    state_ref,
    quantized_ref,
    wide_ref,
    levels_ref,
    centres_ref,
    bias_ref,
    projection_ref,
    sems,
):
    first = (lax.axis_index("z") == 0) & (lax.axis_index("x") == 0)
    copy_all(
        [
            (weight_any.at[:, 0], wide_ref.at[:, :, 0:CH]),
            (weight_any.at[:, 1], wide_ref.at[:, :, CH : 2 * CH]),
            (weight_any.at[:, 2], wide_ref.at[:, :, 2 * CH : 3 * CH]),
            (levels_any, levels_ref),
            (centres_any, centres_ref),
            (bias_any, bias_ref),
            (projection_any, projection_ref.at[0:L]),
        ],
        sems,
    )
    projection_ref[L:8] = jnp.zeros((8 - L, CH), f32)
    rows, columns, groups = centres_ref.shape
    channel = lax.broadcasted_iota(jnp.int32, (columns, groups), 0) % L
    half = half_ranges(levels_ref, channel)
    for h in range(rows):
        quantized_ref[h] = (centres_ref[h].astype(f32) - half) / half

    @pl.when(first)
    def _():
        for t in range(2):
            early_ref[t] = x_ref[0]

    @pl.when(jnp.logical_not(first))
    def _():
        early_ref[...] = earlier_ref[...]

    block = block_of(early_ref, x_ref)

    wide = wide_ref[...].reshape(9 * CH, 3 * CH)
    bias = bias_ref[...]
    pooled = [jnp.zeros((W, CH), f32) for _ in range(4)]
    for t in range(4):
        for h in range(4):
            left = jnp.concatenate([block(t + a, h + b) for a in range(3) for b in range(3)], 1)
            z = jnp.dot(left, wide, preferred_element_type=f32)
            preact = (
                bias
                + shifted_rows(z[:, :CH], 1)
                + z[:, CH : 2 * CH]
                + shifted_rows(z[:, 2 * CH :], -1)
            )
            sigmoid = 1.0 / (1.0 + jnp.exp(-preact))
            place = (t * 4 + h) * W
            state_ref[place : place + W] = sigmoid * (1.0 + preact * (1.0 - sigmoid))
            pooled[h] = pooled[h] + (preact * sigmoid).astype(bf16).astype(f32)
    pooled = jnp.concatenate(pooled, 0) * 0.25
    state_ref[STATE : STATE + 4 * W] = pooled
    projection = projection_ref[...]
    latent = lax.dot_general(
        projection, pooled, (((1,), (1,)), ((), ())), precision=highest, preferred_element_type=f32
    )
    squashed = jnp.tanh(latent)
    for h in range(4):
        state_ref[SMALL + 8 * h : SMALL + 8 * h + 8] = squashed[:, h * W : (h + 1) * W]
    state_ref[SMALL + 32 : SMALL + 40] = projection
    channel = lax.broadcasted_iota(jnp.int32, (8, CH), 0)
    state_ref[SMALL + 40 : SMALL + 48] = half_ranges(levels_ref, channel)


def window(early_ref, x_ref, a, b):
    blocks = []
    if a < 2:
        blocks.append(early_ref[a:2, b : b + 4].reshape((2 - a) * 4 * W, CH))
    if a > 0:
        blocks.append(x_ref[max(a - 2, 0) : a + 2, b : b + 4].reshape(-1, CH))
    else:
        blocks.append(x_ref[0:2, b : b + 4].reshape(8 * W, CH))
    return jnp.concatenate(blocks, 0) if len(blocks) > 1 else blocks[0]


def backward_kernel(
    total_cells,
    early_ref,
    x_ref,
    state_ref,
    code_ref,
    mine_ref,
    theirs_ref,
    low_ref,
    grad_ref,
):
    core = lax.axis_index("c")
    pooled = state_ref[STATE : STATE + 4 * W]
    squashed = jnp.concatenate(
        [state_ref[SMALL + 8 * h : SMALL + 8 * h + 8] for h in range(4)], 1
    )
    projection = state_ref[SMALL + 32 : SMALL + 40]
    half = state_ref[SMALL + 40 : SMALL + 48]
    tile_of = lax.broadcasted_iota(jnp.int32, (W, 32), 1)
    column = lax.broadcasted_iota(jnp.int32, (W, 32), 0)
    spread = jnp.where(column // 4 == tile_of, 1.0, 0.0).astype(f32)
    repeated = jnp.dot(spread, code_ref[...], precision=highest, preferred_element_type=f32)
    place = lax.broadcasted_iota(jnp.int32, (W, CH), 1)
    column = lax.broadcasted_iota(jnp.int32, (W, CH), 0)
    repeated = jnp.where((place % 24) // L == column % 4, repeated, 0.0)
    wanted = lax.broadcasted_iota(jnp.int32, (32, CH), 0)
    place = lax.broadcasted_iota(jnp.int32, (32, CH), 1)
    pick = jnp.where((place // 24 == wanted // 8) & (place % L == wanted % 8), 1.0, 0.0).astype(f32)
    codes = lax.dot_general(
        pick, repeated, (((1,), (1,)), ((), ())), precision=highest, preferred_element_type=f32
    )
    codes = jnp.concatenate([codes[8 * h : 8 * h + 8] / half for h in range(4)], 1)
    code_step = (
        (codes + 2.0 * commit_weight * offset_scale * squashed)
        * offset_scale
        * (1.0 - squashed * squashed)
        * float(total_cells) ** (-0.5)
    )
    projection_part = jnp.dot(code_step, pooled, precision=highest, preferred_element_type=f32)
    pooled_grad = 0.25 * lax.dot_general(
        code_step, projection, (((0,), (0,)), ((), ())), precision=highest, preferred_element_type=f32
    )
    bias_part = jnp.zeros((8, CH), f32)
    for t in range(4):
        for h in range(4):
            place = (t * 4 + h) * W
            pre_grad = pooled_grad[h * W : (h + 1) * W] * state_ref[place : place + W]
            bias_part = bias_part + pre_grad.reshape(W // 8, 8, CH).sum(0)
            turned = pre_grad.T
            low_ref[0:CH, place : place + W] = shifted_lanes(turned, -1).astype(bf16)
            low_ref[CH : 2 * CH, place : place + W] = turned.astype(bf16)
            low_ref[2 * CH :, place : place + W] = shifted_lanes(turned, 1).astype(bf16)
    bias_row = bias_part.sum(0, keepdims=True)
    row = lax.broadcasted_iota(jnp.int32, (8, CH), 0)
    small = jnp.where(row == L, bias_row, projection_part)
    taps = [(a, b) for a in range(3) for b in range(3)]
    for start in range(0, 9, 2):
        group = taps[start : start + 2]
        right = jnp.concatenate([window(early_ref, x_ref, a, b) for a, b in group], 1)
        grad_ref[:, start * CH : (start + len(group)) * CH] = jnp.dot(
            low_ref[...], right, preferred_element_type=f32
        )
    for y in range(4):
        for c in range(3):
            own = pl.multiple_of(c * CH + 32 * y + 16 * core, 16)
            other = pl.multiple_of(c * CH + 32 * y + 16 * (1 - core), 16)
            for tap in range(9):
                to = slice((3 * tap + c) * CH, (3 * tap + c + 1) * CH)
                mine_ref[y, :, to] = grad_ref[pl.ds(own, 16), tap * CH : (tap + 1) * CH]
                theirs_ref[y, :, to] = grad_ref[pl.ds(other, 16), tap * CH : (tap + 1) * CH]
        mine_ref[y, 0:8, LANES:] = small
        mine_ref[y, 8:16, LANES:] = jnp.zeros((8, CH), f32)
        theirs_ref[y, 0:8, LANES:] = small
        theirs_ref[y, 8:16, LANES:] = jnp.zeros((8, CH), f32)


def pair_kernel(mine_ref, got_ref, out_ref):
    small = mine_ref[0, 0:8, LANES:] + got_ref[0, 0:8, LANES:]
    high = small.astype(bf16).astype(f32)
    small = jnp.concatenate([high, small - high], 0).astype(bf16)
    share = LANES // 32
    for y in range(4):
        for k in range(32):
            start = k * share
            base = start // CH * CH
            window = mine_ref[y, :, base : base + 2 * CH] + got_ref[y, :, base : base + 2 * CH]
            if start > base:
                window = pltpu.roll(window, 2 * CH - (start - base), 1)
            z, x = divmod(k, 4)
            out_ref[x * 4 + y, z * 16 : (z + 1) * 16] = window[:, :CH].astype(bf16)
        for x in range(4):
            out_ref[x * 4 + y, 128:144] = small


def plane_kernel(parts_ref, out_ref):
    total = parts_ref[0].astype(f32)
    for k in range(1, parts_ref.shape[0]):
        total = total + parts_ref[k].astype(f32)
    small = total[128:136] + total[136:144]
    for z in range(8):
        out_ref[z, 0:16] = total[z * 16 : (z + 1) * 16]
        out_ref[z, 16:24] = small


def final_kernel(parts_ref, weight_ref, projection_ref, bias_ref):
    total = parts_ref[0]
    for k in range(1, parts_ref.shape[0]):
        total = total + parts_ref[k]
    weight_ref[...] = total[0:16, : weight_ref.shape[1]]
    projection_ref[...] = total[16 : 16 + L]
    bias_ref[...] = total[16 + L : 17 + L]


def on_device(frames, conv_weight, conv_bias, projection, levels, centres, code_grad):
    time_axes, row_axes, all_axes = ("z", "x"), ("y", "c"), ("z", "x", "y", "c")
    shards = 32
    strips = 8
    shape = jax.ShapeDtypeStruct
    dma = pltpu.SemaphoreType.DMA

    code_grad = jnp.transpose(code_grad, (1, 2, 0))
    centres = jnp.transpose(centres, (1, 2, 0))
    lower = [(i, i + 1) for i in range(strips - 1)]
    edge = shape((4, W, CH), bf16)
    own = shape((4, 6, W, CH), bf16)
    x, top, bottom = call(edge_kernel, [own, edge, edge], [ANY], [dma((3,))])(frames)
    up = lax.ppermute(bottom, row_axes, lower)
    down = lax.ppermute(top, row_axes, [(b, a) for a, b in lower])
    (codes,) = call(code_kernel, [shape((shards, CH), f32)], [VMEM])(code_grad)
    codes = lax.all_to_all(codes.reshape(shards, 1, CH), time_axes, 0, 0, tiled=True)
    codes = codes.reshape(shards, CH)
    x, late = call(
        late_kernel, [own, shape((2, 6, W, CH), bf16)], [VMEM] * 3, aliases={0: 0}
    )(x, up, down)
    earlier = lax.ppermute(late, time_axes, [(i, i + 1) for i in range(shards - 1)])
    early, state, quantized = call(
        forward_kernel,
        [shape((2, 6, W, CH), bf16), shape((SMALL + 48, CH), f32), shape(centres.shape, f32)],
        [ANY] * 2 + [VMEM] * 2 + [ANY] * 3,
        [
            pltpu.VMEM((9, CH, 3 * CH), bf16),
            pltpu.SMEM((L,), jnp.int32),
            pltpu.VMEM(centres.shape, jnp.int32),
            pltpu.VMEM((1, CH), f32),
            pltpu.VMEM((8, CH), f32),
            dma((7,)),
        ],
    )(
        levels,
        centres,
        earlier,
        x,
        conv_weight.reshape(9, 3, CH, CH),
        conv_bias.reshape(1, CH),
        projection.T,
    )

    total_cells = 4 * shards * 4 * strips * W
    mine, theirs = call(
        lambda *refs: backward_kernel(total_cells, *refs),
        [shape((4, 16, WIDE), f32)] * 2,
        [VMEM] * 4,
        [pltpu.VMEM((3 * CH, 16 * W), bf16), pltpu.VMEM((3 * CH, 9 * CH), f32)],
    )(early, x, state, codes)

    got = lax.ppermute(theirs, "c", [(0, 1), (1, 0)])
    (chunks,) = call(pair_kernel, [shape((16, 144, CH), bf16)], [VMEM] * 2)(mine, got)
    chunks = lax.all_to_all(chunks, ("x", "y"), 0, 0, tiled=True)
    (chunks,) = call(plane_kernel, [shape((8, 24, CH), f32)], [VMEM])(chunks)
    parts = lax.all_to_all(chunks, "z", 0, 0, tiled=True)
    weight_grad, projection_grad, bias_grad = call(
        final_kernel,
        [shape((16, LANES // shards), f32), shape((L, CH), f32), shape((1, CH), f32)],
        [VMEM],
    )(parts)
    quantized = jnp.transpose(quantized, (2, 0, 1))
    return quantized, weight_grad.T, projection_grad.T, bias_grad.reshape(CH)


def solution(mesh):
    mesh = jax.sharding.Mesh(mesh.devices.reshape(8, 4, 4, 2), ("z", "x", "y", "c"))
    time, rows = ("z", "x"), ("y", "c")
    return jax.shard_map(
        on_device,
        mesh=mesh,
        in_specs=(
            P(time, rows, None, None),
            P(),
            P(),
            P(),
            P(),
            P(None, rows, time),
            P(None, rows, time),
        ),
        out_specs=(P(None, rows, time), P(time, rows), P(), P()),
        check_vma=False,
    )
```

```python
import jax
import jax.numpy as jnp
from jax import lax
from jax.experimental import pallas as pl
from jax.experimental.pallas import tpu as pltpu
from jax.sharding import PartitionSpec as P

offset_scale = 0.45
commit_weight = 0.25
highest = lax.Precision.HIGHEST
bf16 = jnp.bfloat16
f32 = jnp.float32
MIB = 1024 * 1024
CH = 128
L = 6
W = 128
TAPS = 27
LANES = TAPS * CH
WIDE = LANES + CH
STATE = 16 * W
SMALL = 20 * W


VMEM = pl.BlockSpec(memory_space=pltpu.VMEM)
ANY = pl.BlockSpec(memory_space=pl.ANY)


def call(kernel, out_shape, in_specs, scratch=(), aliases=None):
    return pl.pallas_call(
        kernel,
        out_shape=out_shape,
        in_specs=in_specs,
        out_specs=[VMEM] * len(out_shape),
        scratch_shapes=list(scratch),
        input_output_aliases=aliases or {},
        compiler_params=pltpu.CompilerParams(vmem_limit_bytes=24 * MIB),
    )


def copy_all(pairs, sems):
    copies = [pltpu.make_async_copy(src, dst, sems.at[i]) for i, (src, dst) in enumerate(pairs)]
    for copy in copies:
        copy.start()
    for copy in copies:
        copy.wait()


def half_ranges(levels_ref, channel):
    half = jnp.ones(channel.shape, f32)
    for j in range(L):
        half = jnp.where(channel == j, (levels_ref[:, j : j + 1].astype(f32) - 1.0) * 0.5, half)
    return half


def code_kernel(grad_ref, codes_ref):
    rows, columns, frames = grad_ref.shape
    stacked = jnp.concatenate([grad_ref[h] for h in range(rows)], 0)
    padded = jnp.pad(stacked, ((0, CH - rows * columns), (0, CH - frames)))
    codes_ref[...] = padded.T[:frames]


def edge_kernel(frames_any, x_ref, inner_ref, outer_ref, sems):
    core = lax.axis_index("c")
    copy_all(
        [
            (frames_any, x_ref.at[:, 1:5]),
            (frames_any.at[:, 3 - 3 * core], inner_ref),
            (frames_any.at[:, 3 * core], outer_ref),
        ],
        sems,
    )


def late_kernel(own_ref, inner_ref, outer_ref, code_any, x_ref, late_ref):
    core = lax.axis_index("c")
    inner_row, outer_row = 5 - 5 * core, 5 * core
    for t in range(4):
        x_ref[t, inner_row] = inner_ref[t]
        x_ref[t, outer_row] = outer_ref[t]
    for t in range(2):
        late_ref[t, inner_row] = inner_ref[t + 2]
        late_ref[t, outer_row] = outer_ref[t + 2]
        for h in range(1, 5):
            late_ref[t, h] = own_ref[t + 2, h]


def early_kernel(earlier_ref, x_ref, early_ref):
    first = (lax.axis_index("z") == 0) & (lax.axis_index("x") == 0)

    @pl.when(first)
    def _():
        for t in range(2):
            early_ref[t] = x_ref[0]

    @pl.when(jnp.logical_not(first))
    def _():
        early_ref[...] = earlier_ref[...]


def block_of(early_ref, x_ref):
    return lambda t, h: early_ref[t, h] if t < 2 else x_ref[t - 2, h]


def shifted_rows(value, step):
    row = lax.broadcasted_iota(jnp.int32, value.shape, 0)
    rolled = pltpu.roll(value, step % value.shape[0], 0)
    edge = 0 if step == 1 else value.shape[0] - 1
    return jnp.where(row == edge, 0.0, rolled)


def shifted_lanes(value, step):
    lane = lax.broadcasted_iota(jnp.int32, value.shape, 1)
    rolled = pltpu.roll(value, step % value.shape[1], 1)
    edge = 0 if step == 1 else value.shape[1] - 1
    return jnp.where(lane == edge, 0.0, rolled)


def forward_kernel(
    levels_ref,
    centres_ref,
    early_ref,
    x_ref,
    weight_ref,
    bias_ref,
    projection_ref,
    state_ref,
    quantized_ref,
):
    rows, columns, groups = centres_ref.shape
    channel = lax.broadcasted_iota(jnp.int32, (columns, groups), 0) % L
    half = half_ranges(levels_ref, channel)
    for h in range(rows):
        quantized_ref[h] = (centres_ref[h].astype(f32) - half) / half

    block = block_of(early_ref, x_ref)

    wide = jnp.concatenate(
        [jnp.concatenate([weight_ref[tap, c] for c in range(3)], 1) for tap in range(9)], 0
    )
    bias = bias_ref[...]
    pooled = [jnp.zeros((W, CH), f32) for _ in range(4)]
    for t in range(4):
        for h in range(4):
            left = jnp.concatenate([block(t + a, h + b) for a in range(3) for b in range(3)], 1)
            z = jnp.dot(left, wide, preferred_element_type=f32)
            preact = (
                bias
                + shifted_rows(z[:, :CH], 1)
                + z[:, CH : 2 * CH]
                + shifted_rows(z[:, 2 * CH :], -1)
            )
            sigmoid = 0.5 * jnp.tanh(0.5 * preact) + 0.5
            place = (t * 4 + h) * W
            state_ref[place : place + W] = sigmoid * (1.0 + preact * (1.0 - sigmoid))
            pooled[h] = pooled[h] + (preact * sigmoid).astype(bf16).astype(f32)
    pooled = jnp.concatenate(pooled, 0) * 0.25
    state_ref[STATE : STATE + 4 * W] = pooled
    projection = jnp.concatenate([projection_ref[...], jnp.zeros((8 - L, CH), f32)], 0)
    latent = lax.dot_general(
        projection, pooled, (((1,), (1,)), ((), ())), precision=highest, preferred_element_type=f32
    )
    squashed = jnp.tanh(latent)
    for h in range(4):
        state_ref[SMALL + 8 * h : SMALL + 8 * h + 8] = squashed[:, h * W : (h + 1) * W]
    state_ref[SMALL + 32 : SMALL + 40] = projection
    channel = lax.broadcasted_iota(jnp.int32, (8, CH), 0)
    state_ref[SMALL + 40 : SMALL + 48] = half_ranges(levels_ref, channel)


def window(early_ref, x_ref, a, b):
    blocks = []
    if a < 2:
        blocks.append(early_ref[a:2, b : b + 4].reshape((2 - a) * 4 * W, CH))
    if a > 0:
        blocks.append(x_ref[max(a - 2, 0) : a + 2, b : b + 4].reshape(-1, CH))
    else:
        blocks.append(x_ref[0:2, b : b + 4].reshape(8 * W, CH))
    return jnp.concatenate(blocks, 0) if len(blocks) > 1 else blocks[0]


def backward_kernel(
    total_cells,
    early_ref,
    x_ref,
    state_ref,
    code_ref,
    theirs_ref,
    low_ref,
    small_ref,
):
    core = lax.axis_index("c")
    pooled = state_ref[STATE : STATE + 4 * W]
    squashed = jnp.concatenate(
        [state_ref[SMALL + 8 * h : SMALL + 8 * h + 8] for h in range(4)], 1
    )
    projection = state_ref[SMALL + 32 : SMALL + 40]
    half = state_ref[SMALL + 40 : SMALL + 48]
    tile_of = lax.broadcasted_iota(jnp.int32, (W, 32), 1)
    column = lax.broadcasted_iota(jnp.int32, (W, 32), 0)
    spread = jnp.where(column // 4 == tile_of, 1.0, 0.0).astype(f32)
    repeated = jnp.dot(spread, code_ref[...], precision=highest, preferred_element_type=f32)
    place = lax.broadcasted_iota(jnp.int32, (W, CH), 1)
    column = lax.broadcasted_iota(jnp.int32, (W, CH), 0)
    repeated = jnp.where((place % 24) // L == column % 4, repeated, 0.0)
    wanted = lax.broadcasted_iota(jnp.int32, (32, CH), 0)
    place = lax.broadcasted_iota(jnp.int32, (32, CH), 1)
    pick = jnp.where((place // 24 == wanted // 8) & (place % L == wanted % 8), 1.0, 0.0).astype(f32)
    codes = lax.dot_general(
        pick, repeated, (((1,), (1,)), ((), ())), precision=highest, preferred_element_type=f32
    )
    codes = jnp.concatenate([codes[8 * h : 8 * h + 8] / half for h in range(4)], 1)
    code_step = (
        (codes + 2.0 * commit_weight * offset_scale * squashed)
        * offset_scale
        * (1.0 - squashed * squashed)
        * float(total_cells) ** (-0.5)
    )
    projection_part = jnp.dot(code_step, pooled, precision=highest, preferred_element_type=f32)
    pooled_grad = 0.25 * lax.dot_general(
        code_step, projection, (((0,), (0,)), ((), ())), precision=highest, preferred_element_type=f32
    )
    bias_part = jnp.zeros((8, CH), f32)
    for t in range(4):
        for h in range(4):
            place = (t * 4 + h) * W
            pre_grad = pooled_grad[h * W : (h + 1) * W] * state_ref[place : place + W]
            bias_part = bias_part + pre_grad.reshape(W // 8, 8, CH).sum(0)
            turned = pre_grad.T
            low_ref[0:CH, place : place + W] = shifted_lanes(turned, -1).astype(bf16)
            low_ref[CH : 2 * CH, place : place + W] = turned.astype(bf16)
            low_ref[2 * CH :, place : place + W] = shifted_lanes(turned, 1).astype(bf16)
    bias_row = bias_part.sum(0, keepdims=True)
    row = lax.broadcasted_iota(jnp.int32, (8, CH), 0)
    small = jnp.where(row == L, bias_row, projection_part)
    small_ref[...] = small
    kernel_gradient(1 - core, early_ref, x_ref, low_ref, theirs_ref)
    for y in range(4):
        theirs_ref[y, 0:8, LANES:] = small
        theirs_ref[y, 8:16, LANES:] = jnp.zeros((8, CH), f32)


def kernel_gradient(core, early_ref, x_ref, low_ref, out_ref):
    starts = [pl.multiple_of(c * CH + 32 * y + 16 * core, 16) for c in range(3) for y in range(4)]
    left = jnp.concatenate([low_ref[pl.ds(start, 16), :] for start in starts], 0)
    taps = [(a, b) for a in range(3) for b in range(3)]
    for start in range(0, 9, 2):
        group = taps[start : start + 2]
        right = jnp.concatenate([window(early_ref, x_ref, a, b) for a, b in group], 1)
        result = jnp.dot(left, right, preferred_element_type=f32)
        for place in range(len(group)):
            for c in range(3):
                to = slice((3 * (start + place) + c) * CH, (3 * (start + place) + c + 1) * CH)
                for y in range(4):
                    row = (c * 4 + y) * 16
                    out_ref[y, :, to] = result[row : row + 16, place * CH : (place + 1) * CH]


def own_kernel(early_ref, x_ref, low_ref, small_ref, mine_ref):
    kernel_gradient(lax.axis_index("c"), early_ref, x_ref, low_ref, mine_ref)
    for y in range(4):
        mine_ref[y, 0:8, LANES:] = small_ref[...]
        mine_ref[y, 8:16, LANES:] = jnp.zeros((8, CH), f32)


def pair_kernel(mine_ref, got_ref, out_ref):
    small = mine_ref[0, 0:8, LANES:] + got_ref[0, 0:8, LANES:]
    high = small.astype(bf16).astype(f32)
    small = jnp.concatenate([high, small - high], 0).astype(bf16)
    share = LANES // 32
    for y in range(4):
        for k in range(32):
            start = k * share
            base = start // CH * CH
            window = mine_ref[y, :, base : base + 2 * CH] + got_ref[y, :, base : base + 2 * CH]
            if start > base:
                window = pltpu.roll(window, 2 * CH - (start - base), 1)
            z, x = divmod(k, 4)
            out_ref[x * 4 + y, z * 16 : (z + 1) * 16] = window[:, :CH].astype(bf16)
        for x in range(4):
            out_ref[x * 4 + y, 128:144] = small


def plane_kernel(parts_ref, out_ref):
    total = parts_ref[0].astype(f32)
    for k in range(1, parts_ref.shape[0]):
        total = total + parts_ref[k].astype(f32)
    small = total[128:136] + total[136:144]
    for z in range(8):
        out_ref[z, 0:16] = total[z * 16 : (z + 1) * 16]
        out_ref[z, 16:24] = small


def final_kernel(parts_ref, weight_ref, projection_ref, bias_ref):
    total = parts_ref[0]
    for k in range(1, parts_ref.shape[0]):
        total = total + parts_ref[k]
    weight_ref[...] = total[0:16, : weight_ref.shape[1]]
    projection_ref[...] = total[16 : 16 + L]
    bias_ref[...] = total[16 + L : 17 + L]


def on_device(frames, conv_weight, conv_bias, projection, levels, centres, code_grad):
    time_axes, row_axes, all_axes = ("z", "x"), ("y", "c"), ("z", "x", "y", "c")
    shards = 32
    strips = 8
    shape = jax.ShapeDtypeStruct
    dma = pltpu.SemaphoreType.DMA

    code_grad = jnp.transpose(code_grad, (1, 2, 0))
    centres = jnp.transpose(centres, (1, 2, 0))
    crossing = [(i, i + 1) for i in range(1, strips - 1, 2)]
    crossing = crossing + [(b, a) for a, b in crossing]
    edge = shape((4, W, CH), bf16)
    own = shape((4, 6, W, CH), bf16)
    x, inner, outer = call(edge_kernel, [own, edge, edge], [ANY], [dma((3,))])(frames)
    outer = lax.ppermute(outer, row_axes, crossing)
    inner = lax.ppermute(inner, "c", [(0, 1), (1, 0)])
    (codes,) = call(code_kernel, [shape((shards, CH), f32)], [VMEM])(code_grad)
    x, late = call(
        late_kernel, [own, shape((2, 6, W, CH), bf16)], [VMEM] * 3 + [ANY], aliases={0: 0}
    )(x, inner, outer, codes)
    codes = lax.all_to_all(codes.reshape(shards, 1, CH), time_axes, 0, 0, tiled=True)
    codes = codes.reshape(shards, CH)
    earlier = lax.ppermute(late, time_axes, [(i, i + 1) for i in range(shards - 1)])
    (early,) = call(early_kernel, [shape((2, 6, W, CH), bf16)], [VMEM] * 2)(earlier, x)
    state, quantized = call(
        forward_kernel,
        [shape((SMALL + 48, CH), f32), shape(centres.shape, f32)],
        [VMEM] * 7,
    )(
        levels.reshape(1, L),
        centres,
        early,
        x,
        conv_weight.reshape(9, 3, CH, CH),
        conv_bias.reshape(1, CH),
        projection.T,
    )

    total_cells = 4 * shards * 4 * strips * W
    theirs, low, small = call(
        lambda *refs: backward_kernel(total_cells, *refs),
        [shape((4, 16, WIDE), f32), shape((3 * CH, 16 * W), bf16), shape((8, CH), f32)],
        [VMEM] * 4,
    )(early, x, state, codes)

    got = lax.ppermute(theirs, "c", [(0, 1), (1, 0)])
    (mine,) = call(own_kernel, [shape((4, 16, WIDE), f32)], [VMEM] * 4)(early, x, low, small)
    (chunks,) = call(pair_kernel, [shape((16, 144, CH), bf16)], [VMEM] * 2)(mine, got)
    chunks = lax.all_to_all(chunks, ("x", "y"), 0, 0, tiled=True)
    (chunks,) = call(plane_kernel, [shape((8, 24, CH), f32)], [VMEM])(chunks)
    parts = lax.all_to_all(chunks, "z", 0, 0, tiled=True)
    weight_grad, projection_grad, bias_grad = call(
        final_kernel,
        [shape((16, LANES // shards), f32), shape((L, CH), f32), shape((1, CH), f32)],
        [VMEM],
    )(parts)
    quantized = jnp.transpose(quantized, (2, 0, 1))
    return quantized, weight_grad.T, projection_grad.T, bias_grad.reshape(CH)


def solution(mesh):
    mesh = jax.sharding.Mesh(mesh.devices.reshape(8, 4, 4, 2), ("z", "x", "y", "c"))
    time, rows = ("z", "x"), ("y", "c")
    return jax.shard_map(
        on_device,
        mesh=mesh,
        in_specs=(
            P(time, rows, None, None),
            P(),
            P(),
            P(),
            P(),
            P(None, rows, time),
            P(None, rows, time),
        ),
        out_specs=(P(None, rows, time), P(time, rows), P(), P()),
        check_vma=False,
    )
```

```python
import jax
import jax.numpy as jnp
from jax import lax
from jax.experimental import pallas as pl
from jax.experimental.pallas import tpu as pltpu
from jax.sharding import PartitionSpec as P

offset_scale = 0.45
commit_weight = 0.25
highest = lax.Precision.HIGHEST
bf16 = jnp.bfloat16
f32 = jnp.float32
MIB = 1024 * 1024
CH = 128
L = 6
W = 128
TAPS = 27
LANES = TAPS * CH
WIDE = LANES + CH
STATE = 16 * W
SMALL = 20 * W


VMEM = pl.BlockSpec(memory_space=pltpu.VMEM)
ANY = pl.BlockSpec(memory_space=pl.ANY)


def call(kernel, out_shape, in_specs, scratch=(), aliases=None):
    return pl.pallas_call(
        kernel,
        out_shape=out_shape,
        in_specs=in_specs,
        out_specs=[VMEM] * len(out_shape),
        scratch_shapes=list(scratch),
        input_output_aliases=aliases or {},
        compiler_params=pltpu.CompilerParams(vmem_limit_bytes=24 * MIB),
    )


def copy_all(pairs, sems):
    copies = [pltpu.make_async_copy(src, dst, sems.at[i]) for i, (src, dst) in enumerate(pairs)]
    for copy in copies:
        copy.start()
    for copy in copies:
        copy.wait()


def half_ranges(levels_ref, channel):
    half = jnp.ones(channel.shape, f32)
    for j in range(L):
        half = jnp.where(channel == j, (levels_ref[:, j : j + 1].astype(f32) - 1.0) * 0.5, half)
    return half


def code_kernel(grad_ref, codes_ref):
    rows, columns, frames = grad_ref.shape
    stacked = jnp.concatenate([grad_ref[h] for h in range(rows)], 0)
    padded = jnp.pad(stacked, ((0, CH - rows * columns), (0, CH - frames)))
    codes_ref[...] = padded.T[:frames]


def edge_kernel(frames_any, x_ref, inner_ref, outer_ref, late_ref, sems):
    core = lax.axis_index("c")
    copy_all(
        [
            (frames_any, x_ref.at[:, 1:5]),
            (frames_any.at[:, 3 - 3 * core], inner_ref),
            (frames_any.at[:, 3 * core], outer_ref),
            (frames_any.at[2:4], late_ref),
        ],
        sems,
    )


def rim_kernel(own_ref, inner_ref, outer_ref, code_any, x_ref, rim_ref):
    core = lax.axis_index("c")
    for t in range(4):
        x_ref[t, 5 - 5 * core] = inner_ref[t]
        x_ref[t, 5 * core] = outer_ref[t]
    for t in range(2):
        rim_ref[t, 1 - core] = inner_ref[t + 2]
        rim_ref[t, core] = outer_ref[t + 2]


def early_kernel(earlier_ref, rim_ref, x_ref, early_ref):
    first = (lax.axis_index("z") == 0) & (lax.axis_index("x") == 0)

    @pl.when(first)
    def _():
        for t in range(2):
            early_ref[t] = x_ref[0]

    @pl.when(jnp.logical_not(first))
    def _():
        for t in range(2):
            early_ref[t, 0] = rim_ref[t, 0]
            early_ref[t, 5] = rim_ref[t, 1]
            for h in range(4):
                early_ref[t, h + 1] = earlier_ref[t, h]


def block_of(early_ref, x_ref):
    return lambda t, h: early_ref[t, h] if t < 2 else x_ref[t - 2, h]


def shifted_rows(value, step):
    row = lax.broadcasted_iota(jnp.int32, value.shape, 0)
    rolled = pltpu.roll(value, step % value.shape[0], 0)
    edge = 0 if step == 1 else value.shape[0] - 1
    return jnp.where(row == edge, 0.0, rolled)


def shifted_lanes(value, step):
    lane = lax.broadcasted_iota(jnp.int32, value.shape, 1)
    rolled = pltpu.roll(value, step % value.shape[1], 1)
    edge = 0 if step == 1 else value.shape[1] - 1
    return jnp.where(lane == edge, 0.0, rolled)


def forward_kernel(
    levels_ref,
    centres_ref,
    early_ref,
    x_ref,
    weight_ref,
    bias_ref,
    projection_ref,
    state_ref,
    quantized_ref,
):
    rows, columns, groups = centres_ref.shape
    channel = lax.broadcasted_iota(jnp.int32, (columns, groups), 0) % L
    half = half_ranges(levels_ref, channel)
    for h in range(rows):
        quantized_ref[h] = (centres_ref[h].astype(f32) - half) / half

    block = block_of(early_ref, x_ref)

    wide = jnp.concatenate(
        [jnp.concatenate([weight_ref[tap, c] for c in range(3)], 1) for tap in range(9)], 0
    )
    bias = bias_ref[...]
    pooled = [jnp.zeros((W, CH), f32) for _ in range(4)]
    for t in range(4):
        for h in range(4):
            left = jnp.concatenate([block(t + a, h + b) for a in range(3) for b in range(3)], 1)
            z = jnp.dot(left, wide, preferred_element_type=f32)
            preact = (
                bias
                + shifted_rows(z[:, :CH], 1)
                + z[:, CH : 2 * CH]
                + shifted_rows(z[:, 2 * CH :], -1)
            )
            sigmoid = 0.5 * jnp.tanh(0.5 * preact) + 0.5
            place = (t * 4 + h) * W
            state_ref[place : place + W] = sigmoid * (1.0 + preact * (1.0 - sigmoid))
            pooled[h] = pooled[h] + (preact * sigmoid).astype(bf16).astype(f32)
    pooled = jnp.concatenate(pooled, 0) * 0.25
    state_ref[STATE : STATE + 4 * W] = pooled
    projection = jnp.concatenate([projection_ref[...], jnp.zeros((8 - L, CH), f32)], 0)
    latent = lax.dot_general(
        projection, pooled, (((1,), (1,)), ((), ())), precision=highest, preferred_element_type=f32
    )
    squashed = jnp.tanh(latent)
    for h in range(4):
        state_ref[SMALL + 8 * h : SMALL + 8 * h + 8] = squashed[:, h * W : (h + 1) * W]
    state_ref[SMALL + 32 : SMALL + 40] = projection
    channel = lax.broadcasted_iota(jnp.int32, (8, CH), 0)
    state_ref[SMALL + 40 : SMALL + 48] = half_ranges(levels_ref, channel)


def window(early_ref, x_ref, a, b):
    blocks = []
    if a < 2:
        blocks.append(early_ref[a:2, b : b + 4].reshape((2 - a) * 4 * W, CH))
    if a > 0:
        blocks.append(x_ref[max(a - 2, 0) : a + 2, b : b + 4].reshape(-1, CH))
    else:
        blocks.append(x_ref[0:2, b : b + 4].reshape(8 * W, CH))
    return jnp.concatenate(blocks, 0) if len(blocks) > 1 else blocks[0]


def backward_kernel(
    total_cells,
    early_ref,
    x_ref,
    state_ref,
    code_ref,
    theirs_ref,
    low_ref,
    small_ref,
):
    core = lax.axis_index("c")
    pooled = state_ref[STATE : STATE + 4 * W]
    squashed = jnp.concatenate(
        [state_ref[SMALL + 8 * h : SMALL + 8 * h + 8] for h in range(4)], 1
    )
    projection = state_ref[SMALL + 32 : SMALL + 40]
    half = state_ref[SMALL + 40 : SMALL + 48]
    tile_of = lax.broadcasted_iota(jnp.int32, (W, 32), 1)
    column = lax.broadcasted_iota(jnp.int32, (W, 32), 0)
    spread = jnp.where(column // 4 == tile_of, 1.0, 0.0).astype(f32)
    repeated = jnp.dot(spread, code_ref[...], precision=highest, preferred_element_type=f32)
    place = lax.broadcasted_iota(jnp.int32, (W, CH), 1)
    column = lax.broadcasted_iota(jnp.int32, (W, CH), 0)
    repeated = jnp.where((place % 24) // L == column % 4, repeated, 0.0)
    wanted = lax.broadcasted_iota(jnp.int32, (32, CH), 0)
    place = lax.broadcasted_iota(jnp.int32, (32, CH), 1)
    pick = jnp.where((place // 24 == wanted // 8) & (place % L == wanted % 8), 1.0, 0.0).astype(f32)
    codes = lax.dot_general(
        pick, repeated, (((1,), (1,)), ((), ())), precision=highest, preferred_element_type=f32
    )
    codes = jnp.concatenate([codes[8 * h : 8 * h + 8] / half for h in range(4)], 1)
    code_step = (
        (codes + 2.0 * commit_weight * offset_scale * squashed)
        * offset_scale
        * (1.0 - squashed * squashed)
        * float(total_cells) ** (-0.5)
    )
    projection_part = jnp.dot(code_step, pooled, precision=highest, preferred_element_type=f32)
    pooled_grad = 0.25 * lax.dot_general(
        code_step, projection, (((0,), (0,)), ((), ())), precision=highest, preferred_element_type=f32
    )
    bias_part = jnp.zeros((8, CH), f32)
    for t in range(4):
        for h in range(4):
            place = (t * 4 + h) * W
            pre_grad = pooled_grad[h * W : (h + 1) * W] * state_ref[place : place + W]
            bias_part = bias_part + pre_grad.reshape(W // 8, 8, CH).sum(0)
            turned = pre_grad.T
            low_ref[0:CH, place : place + W] = shifted_lanes(turned, -1).astype(bf16)
            low_ref[CH : 2 * CH, place : place + W] = turned.astype(bf16)
            low_ref[2 * CH :, place : place + W] = shifted_lanes(turned, 1).astype(bf16)
    bias_row = bias_part.sum(0, keepdims=True)
    row = lax.broadcasted_iota(jnp.int32, (8, CH), 0)
    small = jnp.where(row == L, bias_row, projection_part)
    small_ref[...] = small
    kernel_gradient(1 - core, early_ref, x_ref, low_ref, theirs_ref)
    for y in range(4):
        theirs_ref[y, 0:8, LANES:] = small
        theirs_ref[y, 8:16, LANES:] = jnp.zeros((8, CH), f32)


def kernel_gradient(core, early_ref, x_ref, low_ref, out_ref):
    starts = [pl.multiple_of(c * CH + 32 * y + 16 * core, 16) for c in range(3) for y in range(4)]
    left = jnp.concatenate([low_ref[pl.ds(start, 16), :] for start in starts], 0)
    taps = [(a, b) for a in range(3) for b in range(3)]
    for start in range(0, 9, 2):
        group = taps[start : start + 2]
        right = jnp.concatenate([window(early_ref, x_ref, a, b) for a, b in group], 1)
        result = jnp.dot(left, right, preferred_element_type=f32)
        for place in range(len(group)):
            for c in range(3):
                to = slice((3 * (start + place) + c) * CH, (3 * (start + place) + c + 1) * CH)
                for y in range(4):
                    row = (c * 4 + y) * 16
                    out_ref[y, :, to] = result[row : row + 16, place * CH : (place + 1) * CH]


def own_kernel(early_ref, x_ref, low_ref, small_ref, mine_ref):
    kernel_gradient(lax.axis_index("c"), early_ref, x_ref, low_ref, mine_ref)
    for y in range(4):
        mine_ref[y, 0:8, LANES:] = small_ref[...]
        mine_ref[y, 8:16, LANES:] = jnp.zeros((8, CH), f32)


def pair_kernel(mine_ref, got_ref, out_ref):
    small = mine_ref[0, 0:8, LANES:] + got_ref[0, 0:8, LANES:]
    high = small.astype(bf16).astype(f32)
    small = jnp.concatenate([high, small - high], 0).astype(bf16)
    share = LANES // 32
    for y in range(4):
        for k in range(32):
            start = k * share
            base = start // CH * CH
            window = mine_ref[y, :, base : base + 2 * CH] + got_ref[y, :, base : base + 2 * CH]
            if start > base:
                window = pltpu.roll(window, 2 * CH - (start - base), 1)
            z, x = divmod(k, 4)
            out_ref[x * 4 + y, z * 16 : (z + 1) * 16] = window[:, :CH].astype(bf16)
        for x in range(4):
            out_ref[x * 4 + y, 128:144] = small


def plane_kernel(parts_ref, out_ref):
    total = parts_ref[0].astype(f32)
    for k in range(1, parts_ref.shape[0]):
        total = total + parts_ref[k].astype(f32)
    small = total[128:136] + total[136:144]
    for z in range(8):
        out_ref[z, 0:16] = total[z * 16 : (z + 1) * 16]
        out_ref[z, 16:24] = small


def final_kernel(parts_ref, weight_ref, projection_ref, bias_ref):
    total = parts_ref[0]
    for k in range(1, parts_ref.shape[0]):
        total = total + parts_ref[k]
    weight_ref[...] = total[0:16, : weight_ref.shape[1]]
    projection_ref[...] = total[16 : 16 + L]
    bias_ref[...] = total[16 + L : 17 + L]


def on_device(frames, conv_weight, conv_bias, projection, levels, centres, code_grad):
    time_axes, row_axes, all_axes = ("z", "x"), ("y", "c"), ("z", "x", "y", "c")
    shards = 32
    strips = 8
    shape = jax.ShapeDtypeStruct
    dma = pltpu.SemaphoreType.DMA

    code_grad = jnp.transpose(code_grad, (1, 2, 0))
    centres = jnp.transpose(centres, (1, 2, 0))
    crossing = [(i, i + 1) for i in range(1, strips - 1, 2)]
    crossing = crossing + [(b, a) for a, b in crossing]
    edge = shape((4, W, CH), bf16)
    own = shape((4, 6, W, CH), bf16)
    later = [(i, i + 1) for i in range(shards - 1)]
    x, inner, outer, late = call(
        edge_kernel, [own, edge, edge, shape((2, 4, W, CH), bf16)], [ANY], [dma((4,))]
    )(frames)
    earlier = lax.ppermute(late, time_axes, later)
    outer = lax.ppermute(outer, row_axes, crossing)
    inner = lax.ppermute(inner, "c", [(0, 1), (1, 0)])
    (codes,) = call(code_kernel, [shape((shards, CH), f32)], [VMEM])(code_grad)
    x, rim = call(
        rim_kernel, [own, shape((2, 2, W, CH), bf16)], [VMEM] * 3 + [ANY], aliases={0: 0}
    )(x, inner, outer, codes)
    rim = lax.ppermute(rim, time_axes, later)
    codes = lax.all_to_all(codes.reshape(shards, 1, CH), time_axes, 0, 0, tiled=True)
    codes = codes.reshape(shards, CH)
    (early,) = call(early_kernel, [shape((2, 6, W, CH), bf16)], [VMEM] * 3)(earlier, rim, x)
    state, quantized = call(
        forward_kernel,
        [shape((SMALL + 48, CH), f32), shape(centres.shape, f32)],
        [VMEM] * 7,
    )(
        levels.reshape(1, L),
        centres,
        early,
        x,
        conv_weight.reshape(9, 3, CH, CH),
        conv_bias.reshape(1, CH),
        projection.T,
    )

    total_cells = 4 * shards * 4 * strips * W
    theirs, low, small = call(
        lambda *refs: backward_kernel(total_cells, *refs),
        [shape((4, 16, WIDE), f32), shape((3 * CH, 16 * W), bf16), shape((8, CH), f32)],
        [VMEM] * 4,
    )(early, x, state, codes)

    got = lax.ppermute(theirs, "c", [(0, 1), (1, 0)])
    (mine,) = call(own_kernel, [shape((4, 16, WIDE), f32)], [VMEM] * 4)(early, x, low, small)
    (chunks,) = call(pair_kernel, [shape((16, 144, CH), bf16)], [VMEM] * 2)(mine, got)
    chunks = lax.all_to_all(chunks, ("x", "y"), 0, 0, tiled=True)
    (chunks,) = call(plane_kernel, [shape((8, 24, CH), f32)], [VMEM])(chunks)
    parts = lax.all_to_all(chunks, "z", 0, 0, tiled=True)
    weight_grad, projection_grad, bias_grad = call(
        final_kernel,
        [shape((16, LANES // shards), f32), shape((L, CH), f32), shape((1, CH), f32)],
        [VMEM],
    )(parts)
    quantized = jnp.transpose(quantized, (2, 0, 1))
    return quantized, weight_grad.T, projection_grad.T, bias_grad.reshape(CH)


def solution(mesh):
    mesh = jax.sharding.Mesh(mesh.devices.reshape(8, 4, 4, 2), ("z", "x", "y", "c"))
    time, rows = ("z", "x"), ("y", "c")
    return jax.shard_map(
        on_device,
        mesh=mesh,
        in_specs=(
            P(time, rows, None, None),
            P(),
            P(),
            P(),
            P(),
            P(None, rows, time),
            P(None, rows, time),
        ),
        out_specs=(P(None, rows, time), P(time, rows), P(), P()),
        check_vma=False,
    )
```

```python
import jax
import jax.numpy as jnp
from jax import lax
from jax.experimental import pallas as pl
from jax.experimental.pallas import tpu as pltpu
from jax.sharding import PartitionSpec as P

offset_scale = 0.45
commit_weight = 0.25
highest = lax.Precision.HIGHEST
bf16 = jnp.bfloat16
f32 = jnp.float32
MIB = 1024 * 1024
CH = 128
L = 6
W = 128
TAPS = 27
LANES = TAPS * CH
WIDE = LANES + CH
STATE = 16 * W
SMALL = 20 * W


VMEM = pl.BlockSpec(memory_space=pltpu.VMEM)
ANY = pl.BlockSpec(memory_space=pl.ANY)


def call(kernel, out_shape, in_specs, scratch=(), aliases=None):
    return pl.pallas_call(
        kernel,
        out_shape=out_shape,
        in_specs=in_specs,
        out_specs=[VMEM] * len(out_shape),
        scratch_shapes=list(scratch),
        input_output_aliases=aliases or {},
        compiler_params=pltpu.CompilerParams(vmem_limit_bytes=24 * MIB),
    )


def copy_all(pairs, sems):
    copies = [pltpu.make_async_copy(src, dst, sems.at[i]) for i, (src, dst) in enumerate(pairs)]
    for copy in copies:
        copy.start()
    for copy in copies:
        copy.wait()


def half_ranges(levels_ref, channel):
    half = jnp.ones(channel.shape, f32)
    for j in range(L):
        half = jnp.where(channel == j, (levels_ref[:, j : j + 1].astype(f32) - 1.0) * 0.5, half)
    return half


def code_kernel(grad_ref, codes_ref):
    rows, columns, frames = grad_ref.shape
    stacked = jnp.concatenate([grad_ref[h] for h in range(rows)], 0)
    padded = jnp.pad(stacked, ((0, CH - rows * columns), (0, CH - frames)))
    codes_ref[...] = padded.T[:frames]


def edge_kernel(frames_any, x_ref, inner_ref, outer_ref, late_ref, sems):
    core = lax.axis_index("c")
    copy_all(
        [
            (frames_any, x_ref.at[:, 1:5]),
            (frames_any.at[:, 3 - 3 * core], inner_ref),
            (frames_any.at[:, 3 * core], outer_ref),
            (frames_any.at[2:4], late_ref),
        ],
        sems,
    )


def rim_kernel(own_ref, inner_ref, outer_ref, code_any, x_ref, rim_ref):
    core = lax.axis_index("c")
    for t in range(4):
        x_ref[t, 5 - 5 * core] = inner_ref[t]
        x_ref[t, 5 * core] = outer_ref[t]
    for t in range(2):
        rim_ref[t, 1 - core] = inner_ref[t + 2]
        rim_ref[t, core] = outer_ref[t + 2]


def early_kernel(earlier_ref, rim_ref, x_ref, early_ref):
    first = (lax.axis_index("z") == 0) & (lax.axis_index("x") == 0)

    @pl.when(first)
    def _():
        for t in range(2):
            early_ref[t] = x_ref[0]

    @pl.when(jnp.logical_not(first))
    def _():
        for t in range(2):
            early_ref[t, 0] = rim_ref[t, 0]
            early_ref[t, 5] = rim_ref[t, 1]
            for h in range(4):
                early_ref[t, h + 1] = earlier_ref[t, h]


def block_of(early_ref, x_ref):
    return lambda t, h: early_ref[t, h] if t < 2 else x_ref[t - 2, h]


def shifted_rows(value, step):
    row = lax.broadcasted_iota(jnp.int32, value.shape, 0)
    rolled = pltpu.roll(value, step % value.shape[0], 0)
    edge = 0 if step == 1 else value.shape[0] - 1
    return jnp.where(row == edge, 0.0, rolled)


def shifted_lanes(value, step):
    lane = lax.broadcasted_iota(jnp.int32, value.shape, 1)
    rolled = pltpu.roll(value, step % value.shape[1], 1)
    edge = 0 if step == 1 else value.shape[1] - 1
    return jnp.where(lane == edge, 0.0, rolled)


def forward_kernel(
    levels_ref,
    centres_ref,
    early_ref,
    x_ref,
    weight_ref,
    bias_ref,
    projection_ref,
    state_ref,
    quantized_ref,
):
    rows, columns, groups = centres_ref.shape
    channel = lax.broadcasted_iota(jnp.int32, (columns, groups), 0) % L
    half = half_ranges(levels_ref, channel)
    for h in range(rows):
        quantized_ref[h] = (centres_ref[h].astype(f32) - half) / half

    block = block_of(early_ref, x_ref)

    wide = jnp.concatenate(
        [jnp.concatenate([weight_ref[tap, c] for c in range(3)], 1) for tap in range(9)], 0
    )
    bias = bias_ref[...]
    pooled = [jnp.zeros((W, CH), f32) for _ in range(4)]
    for t in range(4):
        for h in range(4):
            left = jnp.concatenate([block(t + a, h + b) for a in range(3) for b in range(3)], 1)
            z = jnp.dot(left, wide, preferred_element_type=f32)
            preact = (
                bias
                + shifted_rows(z[:, :CH], 1)
                + z[:, CH : 2 * CH]
                + shifted_rows(z[:, 2 * CH :], -1)
            )
            sigmoid = 0.5 * jnp.tanh(0.5 * preact) + 0.5
            place = (t * 4 + h) * W
            state_ref[place : place + W] = sigmoid * (1.0 + preact * (1.0 - sigmoid))
            pooled[h] = pooled[h] + (preact * sigmoid).astype(bf16).astype(f32)
    pooled = jnp.concatenate(pooled, 0) * 0.25
    state_ref[STATE : STATE + 4 * W] = pooled
    projection = jnp.concatenate([projection_ref[...], jnp.zeros((8 - L, CH), f32)], 0)
    latent = lax.dot_general(
        projection, pooled, (((1,), (1,)), ((), ())), precision=highest, preferred_element_type=f32
    )
    squashed = jnp.tanh(latent)
    for h in range(4):
        state_ref[SMALL + 8 * h : SMALL + 8 * h + 8] = squashed[:, h * W : (h + 1) * W]
    state_ref[SMALL + 32 : SMALL + 40] = projection
    channel = lax.broadcasted_iota(jnp.int32, (8, CH), 0)
    state_ref[SMALL + 40 : SMALL + 48] = half_ranges(levels_ref, channel)


def window(early_ref, x_ref, a, b):
    blocks = []
    if a < 2:
        blocks.append(early_ref[a:2, b : b + 4].reshape((2 - a) * 4 * W, CH))
    if a > 0:
        blocks.append(x_ref[max(a - 2, 0) : a + 2, b : b + 4].reshape(-1, CH))
    else:
        blocks.append(x_ref[0:2, b : b + 4].reshape(8 * W, CH))
    return jnp.concatenate(blocks, 0) if len(blocks) > 1 else blocks[0]


def backward_kernel(
    total_cells,
    early_ref,
    x_ref,
    state_ref,
    code_ref,
    theirs_ref,
    low_ref,
    small_ref,
):
    core = lax.axis_index("c")
    pooled = state_ref[STATE : STATE + 4 * W]
    squashed = jnp.concatenate(
        [state_ref[SMALL + 8 * h : SMALL + 8 * h + 8] for h in range(4)], 1
    )
    projection = state_ref[SMALL + 32 : SMALL + 40]
    half = state_ref[SMALL + 40 : SMALL + 48]
    tile_of = lax.broadcasted_iota(jnp.int32, (W, 32), 1)
    column = lax.broadcasted_iota(jnp.int32, (W, 32), 0)
    spread = jnp.where(column // 4 == tile_of, 1.0, 0.0).astype(f32)
    repeated = jnp.dot(spread, code_ref[...], precision=highest, preferred_element_type=f32)
    place = lax.broadcasted_iota(jnp.int32, (W, CH), 1)
    column = lax.broadcasted_iota(jnp.int32, (W, CH), 0)
    repeated = jnp.where((place % 24) // L == column % 4, repeated, 0.0)
    wanted = lax.broadcasted_iota(jnp.int32, (32, CH), 0)
    place = lax.broadcasted_iota(jnp.int32, (32, CH), 1)
    pick = jnp.where((place // 24 == wanted // 8) & (place % L == wanted % 8), 1.0, 0.0).astype(f32)
    codes = lax.dot_general(
        pick, repeated, (((1,), (1,)), ((), ())), precision=highest, preferred_element_type=f32
    )
    codes = jnp.concatenate([codes[8 * h : 8 * h + 8] / half for h in range(4)], 1)
    code_step = (
        (codes + 2.0 * commit_weight * offset_scale * squashed)
        * offset_scale
        * (1.0 - squashed * squashed)
        * float(total_cells) ** (-0.5)
    )
    projection_part = jnp.dot(code_step, pooled, precision=highest, preferred_element_type=f32)
    pooled_grad = 0.25 * lax.dot_general(
        code_step, projection, (((0,), (0,)), ((), ())), precision=highest, preferred_element_type=f32
    )
    bias_part = jnp.zeros((8, CH), f32)
    for t in range(4):
        for h in range(4):
            place = (t * 4 + h) * W
            pre_grad = pooled_grad[h * W : (h + 1) * W] * state_ref[place : place + W]
            bias_part = bias_part + pre_grad.reshape(W // 8, 8, CH).sum(0)
            turned = pre_grad.T
            low_ref[0:CH, place : place + W] = shifted_lanes(turned, -1).astype(bf16)
            low_ref[CH : 2 * CH, place : place + W] = turned.astype(bf16)
            low_ref[2 * CH :, place : place + W] = shifted_lanes(turned, 1).astype(bf16)
    bias_row = bias_part.sum(0, keepdims=True)
    row = lax.broadcasted_iota(jnp.int32, (8, CH), 0)
    small = jnp.where(row == L, bias_row, projection_part)
    small_ref[...] = small
    kernel_gradient(1 - core, early_ref, x_ref, low_ref, theirs_ref)
    for y in range(4):
        theirs_ref[y, 0:8, LANES:] = small
        theirs_ref[y, 8:16, LANES:] = jnp.zeros((8, CH), f32)


def kernel_gradient(core, early_ref, x_ref, low_ref, out_ref):
    starts = [pl.multiple_of(c * CH + 32 * y + 16 * core, 16) for c in range(3) for y in range(4)]
    left = jnp.concatenate([low_ref[pl.ds(start, 16), :] for start in starts], 0)
    taps = [(a, b) for a in range(3) for b in range(3)]
    for start in range(0, 9, 2):
        group = taps[start : start + 2]
        right = jnp.concatenate([window(early_ref, x_ref, a, b) for a, b in group], 1)
        result = jnp.dot(left, right, preferred_element_type=f32)
        for place in range(len(group)):
            for c in range(3):
                to = slice((3 * (start + place) + c) * CH, (3 * (start + place) + c + 1) * CH)
                for y in range(4):
                    row = (c * 4 + y) * 16
                    out_ref[y, :, to] = result[row : row + 16, place * CH : (place + 1) * CH]


def own_kernel(early_ref, x_ref, low_ref, small_ref, mine_ref):
    kernel_gradient(lax.axis_index("c"), early_ref, x_ref, low_ref, mine_ref)
    for y in range(4):
        mine_ref[y, 0:8, LANES:] = small_ref[...]
        mine_ref[y, 8:16, LANES:] = jnp.zeros((8, CH), f32)


def pair_kernel(mine_ref, got_ref, out_ref):
    small = mine_ref[0, 0:8, LANES:] + got_ref[0, 0:8, LANES:]
    high = small.astype(bf16).astype(f32)
    small = jnp.concatenate([high, small - high], 0).astype(bf16)
    share = LANES // 32
    for y in range(4):
        total = mine_ref[y, :, :LANES] + got_ref[y, :, :LANES]
        for x in range(4):
            pieces = [
                total[:, (4 * z + x) * share : (4 * z + x + 1) * share] for z in range(8)
            ]
            dense = jnp.concatenate(pieces + [jnp.zeros((16, 7 * CH - 8 * share), f32)], 1)
            out_ref[x * 4 + y, :, : 7 * CH] = dense.astype(bf16)
            out_ref[x * 4 + y, :, 7 * CH :] = small


def plane_kernel(parts_ref, out_ref):
    total = parts_ref[0].astype(f32)
    for k in range(1, parts_ref.shape[0]):
        total = total + parts_ref[k].astype(f32)
    small = total[0:8, 7 * CH :] + total[8:16, 7 * CH :]
    share = LANES // 32
    for z in range(8):
        start = z * share
        base = start // CH * CH
        window = total[:, base : base + 2 * CH]
        if start > base:
            window = pltpu.roll(window, 2 * CH - (start - base), 1)
        out_ref[z, 0:16] = window[:, :CH]
        out_ref[z, 16:24] = small


def final_kernel(parts_ref, weight_ref, projection_ref, bias_ref):
    total = parts_ref[0]
    for k in range(1, parts_ref.shape[0]):
        total = total + parts_ref[k]
    weight_ref[...] = total[0:16, : weight_ref.shape[1]]
    projection_ref[...] = total[16 : 16 + L]
    bias_ref[...] = total[16 + L : 17 + L]


def on_device(frames, conv_weight, conv_bias, projection, levels, centres, code_grad):
    time_axes, row_axes, all_axes = ("z", "x"), ("y", "c"), ("z", "x", "y", "c")
    shards = 32
    strips = 8
    shape = jax.ShapeDtypeStruct
    dma = pltpu.SemaphoreType.DMA

    code_grad = jnp.transpose(code_grad, (1, 2, 0))
    centres = jnp.transpose(centres, (1, 2, 0))
    crossing = [(i, i + 1) for i in range(1, strips - 1, 2)]
    crossing = crossing + [(b, a) for a, b in crossing]
    edge = shape((4, W, CH), bf16)
    own = shape((4, 6, W, CH), bf16)
    later = [(i, i + 1) for i in range(shards - 1)]
    x, inner, outer, late = call(
        edge_kernel, [own, edge, edge, shape((2, 4, W, CH), bf16)], [ANY], [dma((4,))]
    )(frames)
    earlier = lax.ppermute(late, time_axes, later)
    outer = lax.ppermute(outer, row_axes, crossing)
    inner = lax.ppermute(inner, "c", [(0, 1), (1, 0)])
    (codes,) = call(code_kernel, [shape((shards, CH), f32)], [VMEM])(code_grad)
    x, rim = call(
        rim_kernel, [own, shape((2, 2, W, CH), bf16)], [VMEM] * 3 + [ANY], aliases={0: 0}
    )(x, inner, outer, codes)
    rim = lax.ppermute(rim, time_axes, later)
    codes = lax.all_to_all(codes.reshape(shards, 1, CH), time_axes, 0, 0, tiled=True)
    codes = codes.reshape(shards, CH)
    (early,) = call(early_kernel, [shape((2, 6, W, CH), bf16)], [VMEM] * 3)(earlier, rim, x)
    state, quantized = call(
        forward_kernel,
        [shape((SMALL + 48, CH), f32), shape(centres.shape, f32)],
        [VMEM] * 7,
    )(
        levels.reshape(1, L),
        centres,
        early,
        x,
        conv_weight.reshape(9, 3, CH, CH),
        conv_bias.reshape(1, CH),
        projection.T,
    )

    total_cells = 4 * shards * 4 * strips * W
    theirs, low, small = call(
        lambda *refs: backward_kernel(total_cells, *refs),
        [shape((4, 16, WIDE), f32), shape((3 * CH, 16 * W), bf16), shape((8, CH), f32)],
        [VMEM] * 4,
    )(early, x, state, codes)

    got = lax.ppermute(theirs, "c", [(0, 1), (1, 0)])
    (mine,) = call(own_kernel, [shape((4, 16, WIDE), f32)], [VMEM] * 4)(early, x, low, small)
    (chunks,) = call(pair_kernel, [shape((16, 16, 8 * CH), bf16)], [VMEM] * 2)(mine, got)
    chunks = lax.all_to_all(chunks, ("x", "y"), 0, 0, tiled=True)
    (chunks,) = call(plane_kernel, [shape((8, 24, CH), f32)], [VMEM])(chunks)
    parts = lax.all_to_all(chunks, "z", 0, 0, tiled=True)
    weight_grad, projection_grad, bias_grad = call(
        final_kernel,
        [shape((16, LANES // shards), f32), shape((L, CH), f32), shape((1, CH), f32)],
        [VMEM],
    )(parts)
    quantized = jnp.transpose(quantized, (2, 0, 1))
    return quantized, weight_grad.T, projection_grad.T, bias_grad.reshape(CH)


def solution(mesh):
    mesh = jax.sharding.Mesh(mesh.devices.reshape(8, 4, 4, 2), ("z", "x", "y", "c"))
    time, rows = ("z", "x"), ("y", "c")
    return jax.shard_map(
        on_device,
        mesh=mesh,
        in_specs=(
            P(time, rows, None, None),
            P(),
            P(),
            P(),
            P(),
            P(None, rows, time),
            P(None, rows, time),
        ),
        out_specs=(P(None, rows, time), P(time, rows), P(), P()),
        check_vma=False,
    )
```

```python
import jax
import jax.numpy as jnp
from jax import lax
from jax.experimental import pallas as pl
from jax.experimental.pallas import tpu as pltpu
from jax.sharding import PartitionSpec as P

offset_scale = 0.45
commit_weight = 0.25
highest = lax.Precision.HIGHEST
bf16 = jnp.bfloat16
f32 = jnp.float32
MIB = 1024 * 1024
CH = 128
L = 6
W = 128
TAPS = 27
LANES = TAPS * CH
WIDE = LANES + CH
STATE = 16 * W
SMALL = 20 * W


VMEM = pl.BlockSpec(memory_space=pltpu.VMEM)
ANY = pl.BlockSpec(memory_space=pl.ANY)


def call(kernel, out_shape, in_specs, scratch=(), aliases=None):
    return pl.pallas_call(
        kernel,
        out_shape=out_shape,
        in_specs=in_specs,
        out_specs=[VMEM] * len(out_shape),
        scratch_shapes=list(scratch),
        input_output_aliases=aliases or {},
        compiler_params=pltpu.CompilerParams(vmem_limit_bytes=24 * MIB),
    )


def copy_all(pairs, sems):
    copies = [pltpu.make_async_copy(src, dst, sems.at[i]) for i, (src, dst) in enumerate(pairs)]
    for copy in copies:
        copy.start()
    for copy in copies:
        copy.wait()


def half_ranges(levels_ref, channel):
    half = jnp.ones(channel.shape, f32)
    for j in range(L):
        half = jnp.where(channel == j, (levels_ref[:, j : j + 1].astype(f32) - 1.0) * 0.5, half)
    return half


def code_kernel(grad_ref, codes_ref):
    rows, columns, frames = grad_ref.shape
    stacked = jnp.concatenate([grad_ref[h] for h in range(rows)], 0)
    padded = jnp.pad(stacked, ((0, CH - rows * columns), (0, CH - frames)))
    codes_ref[...] = padded.T[:frames]


def edge_kernel(frames_any, x_ref, inner_ref, outer_ref, late_ref, sems):
    core = lax.axis_index("c")
    copy_all(
        [
            (frames_any, x_ref.at[:, 1:5]),
            (frames_any.at[:, 3 - 3 * core], inner_ref),
            (frames_any.at[:, 3 * core], outer_ref),
            (frames_any.at[2:4], late_ref),
        ],
        sems,
    )


def rim_kernel(own_ref, inner_ref, outer_ref, code_any, x_ref, rim_ref):
    core = lax.axis_index("c")
    for t in range(4):
        x_ref[t, 5 - 5 * core] = inner_ref[t]
        x_ref[t, 5 * core] = outer_ref[t]
    for t in range(2):
        rim_ref[t, 1 - core] = inner_ref[t + 2]
        rim_ref[t, core] = outer_ref[t + 2]


def early_kernel(earlier_ref, rim_ref, x_ref, early_ref):
    first = (lax.axis_index("z") == 0) & (lax.axis_index("x") == 0)

    @pl.when(first)
    def _():
        for t in range(2):
            early_ref[t] = x_ref[0]

    @pl.when(jnp.logical_not(first))
    def _():
        for t in range(2):
            early_ref[t, 0] = rim_ref[t, 0]
            early_ref[t, 5] = rim_ref[t, 1]
            for h in range(4):
                early_ref[t, h + 1] = earlier_ref[t, h]


def block_of(early_ref, x_ref):
    return lambda t, h: early_ref[t, h] if t < 2 else x_ref[t - 2, h]


def shifted_rows(value, step):
    row = lax.broadcasted_iota(jnp.int32, value.shape, 0)
    rolled = pltpu.roll(value, step % value.shape[0], 0)
    edge = 0 if step == 1 else value.shape[0] - 1
    return jnp.where(row == edge, 0.0, rolled)


def shifted_lanes(value, step):
    lane = lax.broadcasted_iota(jnp.int32, value.shape, 1)
    rolled = pltpu.roll(value, step % value.shape[1], 1)
    edge = 0 if step == 1 else value.shape[1] - 1
    return jnp.where(lane == edge, 0.0, rolled)


def forward_kernel(
    levels_ref,
    centres_ref,
    early_ref,
    x_ref,
    weight_ref,
    bias_ref,
    projection_ref,
    state_ref,
    quantized_ref,
):
    rows, columns, groups = centres_ref.shape
    channel = lax.broadcasted_iota(jnp.int32, (columns, groups), 0) % L
    half = half_ranges(levels_ref, channel)
    for h in range(rows):
        quantized_ref[h] = (centres_ref[h].astype(f32) - half) / half

    block = block_of(early_ref, x_ref)

    wide = jnp.concatenate(
        [jnp.concatenate([weight_ref[tap, c] for c in range(3)], 1) for tap in range(9)], 0
    )
    bias = bias_ref[...]
    pooled = [jnp.zeros((W, CH), f32) for _ in range(4)]
    for t in range(4):
        for h in range(4):
            left = jnp.concatenate([block(t + a, h + b) for a in range(3) for b in range(3)], 1)
            z = jnp.dot(left, wide, preferred_element_type=f32)
            preact = (
                bias
                + shifted_rows(z[:, :CH], 1)
                + z[:, CH : 2 * CH]
                + shifted_rows(z[:, 2 * CH :], -1)
            )
            sigmoid = 0.5 * jnp.tanh(0.5 * preact) + 0.5
            place = (t * 4 + h) * W
            state_ref[place : place + W] = sigmoid * (1.0 + preact * (1.0 - sigmoid))
            pooled[h] = pooled[h] + (preact * sigmoid).astype(bf16).astype(f32)
    pooled = jnp.concatenate(pooled, 0) * 0.25
    state_ref[STATE : STATE + 4 * W] = pooled
    projection = jnp.concatenate([projection_ref[...], jnp.zeros((8 - L, CH), f32)], 0)
    latent = lax.dot_general(
        projection, pooled, (((1,), (1,)), ((), ())), precision=highest, preferred_element_type=f32
    )
    squashed = jnp.tanh(latent)
    for h in range(4):
        state_ref[SMALL + 8 * h : SMALL + 8 * h + 8] = squashed[:, h * W : (h + 1) * W]
    state_ref[SMALL + 32 : SMALL + 40] = projection
    channel = lax.broadcasted_iota(jnp.int32, (8, CH), 0)
    state_ref[SMALL + 40 : SMALL + 48] = half_ranges(levels_ref, channel)


def window(early_ref, x_ref, a, b):
    blocks = []
    if a < 2:
        blocks.append(early_ref[a:2, b : b + 4].reshape((2 - a) * 4 * W, CH))
    if a > 0:
        blocks.append(x_ref[max(a - 2, 0) : a + 2, b : b + 4].reshape(-1, CH))
    else:
        blocks.append(x_ref[0:2, b : b + 4].reshape(8 * W, CH))
    return jnp.concatenate(blocks, 0) if len(blocks) > 1 else blocks[0]


def backward_kernel(
    total_cells,
    early_ref,
    x_ref,
    state_ref,
    code_ref,
    theirs_ref,
    low_ref,
    small_ref,
):
    core = lax.axis_index("c")
    pooled = state_ref[STATE : STATE + 4 * W]
    squashed = jnp.concatenate(
        [state_ref[SMALL + 8 * h : SMALL + 8 * h + 8] for h in range(4)], 1
    )
    projection = state_ref[SMALL + 32 : SMALL + 40]
    half = state_ref[SMALL + 40 : SMALL + 48]
    tile_of = lax.broadcasted_iota(jnp.int32, (W, 32), 1)
    column = lax.broadcasted_iota(jnp.int32, (W, 32), 0)
    spread = jnp.where(column // 4 == tile_of, 1.0, 0.0).astype(f32)
    repeated = jnp.dot(spread, code_ref[...], precision=highest, preferred_element_type=f32)
    place = lax.broadcasted_iota(jnp.int32, (W, CH), 1)
    column = lax.broadcasted_iota(jnp.int32, (W, CH), 0)
    repeated = jnp.where((place % 24) // L == column % 4, repeated, 0.0)
    wanted = lax.broadcasted_iota(jnp.int32, (32, CH), 0)
    place = lax.broadcasted_iota(jnp.int32, (32, CH), 1)
    pick = jnp.where((place // 24 == wanted // 8) & (place % L == wanted % 8), 1.0, 0.0).astype(f32)
    codes = lax.dot_general(
        pick, repeated, (((1,), (1,)), ((), ())), precision=highest, preferred_element_type=f32
    )
    codes = jnp.concatenate([codes[8 * h : 8 * h + 8] / half for h in range(4)], 1)
    code_step = (
        (codes + 2.0 * commit_weight * offset_scale * squashed)
        * offset_scale
        * (1.0 - squashed * squashed)
        * float(total_cells) ** (-0.5)
    )
    projection_part = jnp.dot(code_step, pooled, precision=highest, preferred_element_type=f32)
    pooled_grad = 0.25 * lax.dot_general(
        code_step, projection, (((0,), (0,)), ((), ())), precision=highest, preferred_element_type=f32
    )
    bias_part = jnp.zeros((8, CH), f32)
    for t in range(4):
        for h in range(4):
            place = (t * 4 + h) * W
            pre_grad = pooled_grad[h * W : (h + 1) * W] * state_ref[place : place + W]
            bias_part = bias_part + pre_grad.reshape(W // 8, 8, CH).sum(0)
            turned = pre_grad.T
            low_ref[0:CH, place : place + W] = shifted_lanes(turned, -1).astype(bf16)
            low_ref[CH : 2 * CH, place : place + W] = turned.astype(bf16)
            low_ref[2 * CH :, place : place + W] = shifted_lanes(turned, 1).astype(bf16)
    bias_row = bias_part.sum(0, keepdims=True)
    row = lax.broadcasted_iota(jnp.int32, (8, CH), 0)
    small = jnp.where(row == L, bias_row, projection_part)
    pieces = split_small(small)
    small_ref[...] = pieces[0:8].astype(f32) + pieces[8:16].astype(f32)
    kernel_gradient(1 - core, early_ref, x_ref, low_ref, theirs_ref)
    for y in range(4):
        theirs_ref[y, :, LANES:] = pieces


def split_small(small):
    high = small.astype(bf16).astype(f32)
    return jnp.concatenate([high, small - high], 0).astype(bf16)


def kernel_gradient(core, early_ref, x_ref, low_ref, out_ref):
    starts = [pl.multiple_of(c * CH + 32 * y + 16 * core, 16) for c in range(3) for y in range(4)]
    left = jnp.concatenate([low_ref[pl.ds(start, 16), :] for start in starts], 0)
    taps = [(a, b) for a in range(3) for b in range(3)]
    for start in range(0, 9, 2):
        group = taps[start : start + 2]
        right = jnp.concatenate([window(early_ref, x_ref, a, b) for a, b in group], 1)
        result = jnp.dot(left, right, preferred_element_type=f32)
        for place in range(len(group)):
            for c in range(3):
                to = slice((3 * (start + place) + c) * CH, (3 * (start + place) + c + 1) * CH)
                for y in range(4):
                    row = (c * 4 + y) * 16
                    part = result[row : row + 16, place * CH : (place + 1) * CH]
                    out_ref[y, :, to] = part.astype(out_ref.dtype)


def own_kernel(early_ref, x_ref, low_ref, small_ref, mine_ref):
    kernel_gradient(lax.axis_index("c"), early_ref, x_ref, low_ref, mine_ref)
    for y in range(4):
        mine_ref[y, 0:8, LANES:] = small_ref[...]
        mine_ref[y, 8:16, LANES:] = jnp.zeros((8, CH), f32)


def pair_kernel(mine_ref, got_ref, out_ref):
    got_small = got_ref[0, :, LANES:].astype(f32)
    small = split_small(mine_ref[0, 0:8, LANES:] + (got_small[0:8] + got_small[8:16]))
    share = LANES // 32
    for y in range(4):
        total = mine_ref[y, :, :LANES] + got_ref[y, :, :LANES].astype(f32)
        for x in range(4):
            pieces = [
                total[:, (4 * z + x) * share : (4 * z + x + 1) * share] for z in range(8)
            ]
            dense = jnp.concatenate(pieces + [jnp.zeros((16, 7 * CH - 8 * share), f32)], 1)
            out_ref[x * 4 + y, :, : 7 * CH] = dense.astype(bf16)
            out_ref[x * 4 + y, :, 7 * CH :] = small


def plane_kernel(parts_ref, out_ref):
    total = parts_ref[0].astype(f32)
    for k in range(1, parts_ref.shape[0]):
        total = total + parts_ref[k].astype(f32)
    small = total[0:8, 7 * CH :] + total[8:16, 7 * CH :]
    share = LANES // 32
    for z in range(8):
        start = z * share
        base = start // CH * CH
        window = total[:, base : base + 2 * CH]
        if start > base:
            window = pltpu.roll(window, 2 * CH - (start - base), 1)
        out_ref[z, 0:16] = window[:, :CH]
        out_ref[z, 16:24] = small


def final_kernel(parts_ref, weight_ref, projection_ref, bias_ref):
    total = parts_ref[0]
    for k in range(1, parts_ref.shape[0]):
        total = total + parts_ref[k]
    weight_ref[...] = total[0:16, : weight_ref.shape[1]]
    projection_ref[...] = total[16 : 16 + L]
    bias_ref[...] = total[16 + L : 17 + L]


def on_device(frames, conv_weight, conv_bias, projection, levels, centres, code_grad):
    time_axes, row_axes, all_axes = ("z", "x"), ("y", "c"), ("z", "x", "y", "c")
    shards = 32
    strips = 8
    shape = jax.ShapeDtypeStruct
    dma = pltpu.SemaphoreType.DMA

    code_grad = jnp.transpose(code_grad, (1, 2, 0))
    centres = jnp.transpose(centres, (1, 2, 0))
    crossing = [(i, i + 1) for i in range(1, strips - 1, 2)]
    crossing = crossing + [(b, a) for a, b in crossing]
    edge = shape((4, W, CH), bf16)
    own = shape((4, 6, W, CH), bf16)
    later = [(i, i + 1) for i in range(shards - 1)]
    x, inner, outer, late = call(
        edge_kernel, [own, edge, edge, shape((2, 4, W, CH), bf16)], [ANY], [dma((4,))]
    )(frames)
    earlier = lax.ppermute(late, time_axes, later)
    outer = lax.ppermute(outer, row_axes, crossing)
    inner = lax.ppermute(inner, "c", [(0, 1), (1, 0)])
    (codes,) = call(code_kernel, [shape((shards, CH), f32)], [VMEM])(code_grad)
    x, rim = call(
        rim_kernel, [own, shape((2, 2, W, CH), bf16)], [VMEM] * 3 + [ANY], aliases={0: 0}
    )(x, inner, outer, codes)
    rim = lax.ppermute(rim, time_axes, later)
    codes = lax.all_to_all(codes.reshape(shards, 1, CH), time_axes, 0, 0, tiled=True)
    codes = codes.reshape(shards, CH)
    (early,) = call(early_kernel, [shape((2, 6, W, CH), bf16)], [VMEM] * 3)(earlier, rim, x)
    state, quantized = call(
        forward_kernel,
        [shape((SMALL + 48, CH), f32), shape(centres.shape, f32)],
        [VMEM] * 7,
    )(
        levels.reshape(1, L),
        centres,
        early,
        x,
        conv_weight.reshape(9, 3, CH, CH),
        conv_bias.reshape(1, CH),
        projection.T,
    )

    total_cells = 4 * shards * 4 * strips * W
    theirs, low, small = call(
        lambda *refs: backward_kernel(total_cells, *refs),
        [shape((4, 16, WIDE), bf16), shape((3 * CH, 16 * W), bf16), shape((8, CH), f32)],
        [VMEM] * 4,
    )(early, x, state, codes)

    got = lax.ppermute(theirs, "c", [(0, 1), (1, 0)])
    (mine,) = call(own_kernel, [shape((4, 16, WIDE), f32)], [VMEM] * 4)(early, x, low, small)
    (chunks,) = call(pair_kernel, [shape((16, 16, 8 * CH), bf16)], [VMEM] * 2)(mine, got)
    chunks = lax.all_to_all(chunks, ("x", "y"), 0, 0, tiled=True)
    (chunks,) = call(plane_kernel, [shape((8, 24, CH), f32)], [VMEM])(chunks)
    parts = lax.all_to_all(chunks, "z", 0, 0, tiled=True)
    weight_grad, projection_grad, bias_grad = call(
        final_kernel,
        [shape((16, LANES // shards), f32), shape((L, CH), f32), shape((1, CH), f32)],
        [VMEM],
    )(parts)
    quantized = jnp.transpose(quantized, (2, 0, 1))
    return quantized, weight_grad.T, projection_grad.T, bias_grad.reshape(CH)


def solution(mesh):
    mesh = jax.sharding.Mesh(mesh.devices.reshape(8, 4, 4, 2), ("z", "x", "y", "c"))
    time, rows = ("z", "x"), ("y", "c")
    return jax.shard_map(
        on_device,
        mesh=mesh,
        in_specs=(
            P(time, rows, None, None),
            P(),
            P(),
            P(),
            P(),
            P(None, rows, time),
            P(None, rows, time),
        ),
        out_specs=(P(None, rows, time), P(time, rows), P(), P()),
        check_vma=False,
    )
```

```python
import jax
import jax.numpy as jnp
from jax import lax
from jax.experimental import pallas as pl
from jax.experimental.pallas import tpu as pltpu
from jax.sharding import PartitionSpec as P

offset_scale = 0.45
commit_weight = 0.25
highest = lax.Precision.HIGHEST
bf16 = jnp.bfloat16
f32 = jnp.float32
MIB = 1024 * 1024
CH = 128
L = 6
W = 128
TAPS = 27
LANES = TAPS * CH
WIDE = LANES + CH
STATE = 16 * W
SMALL = 20 * W


VMEM = pl.BlockSpec(memory_space=pltpu.VMEM)
ANY = pl.BlockSpec(memory_space=pl.ANY)


def call(kernel, out_shape, in_specs, scratch=(), aliases=None):
    return pl.pallas_call(
        kernel,
        out_shape=out_shape,
        in_specs=in_specs,
        out_specs=[VMEM] * len(out_shape),
        scratch_shapes=list(scratch),
        input_output_aliases=aliases or {},
        compiler_params=pltpu.CompilerParams(vmem_limit_bytes=24 * MIB),
    )


def copy_all(pairs, sems):
    copies = [pltpu.make_async_copy(src, dst, sems.at[i]) for i, (src, dst) in enumerate(pairs)]
    for copy in copies:
        copy.start()
    for copy in copies:
        copy.wait()


def half_ranges(levels_ref, channel):
    half = jnp.ones(channel.shape, f32)
    for j in range(L):
        half = jnp.where(channel == j, (levels_ref[:, j : j + 1].astype(f32) - 1.0) * 0.5, half)
    return half


def code_kernel(grad_ref, codes_ref):
    rows, columns, frames = grad_ref.shape
    stacked = jnp.concatenate([grad_ref[h] for h in range(rows)], 0)
    padded = jnp.pad(stacked, ((0, CH - rows * columns), (0, CH - frames)))
    codes_ref[...] = padded.T[:frames]


def edge_kernel(frames_any, x_ref, inner_ref, outer_ref, late_ref, sems):
    core = lax.axis_index("c")
    copy_all(
        [
            (frames_any, x_ref.at[:, 1:5]),
            (frames_any.at[:, 3 - 3 * core], inner_ref),
            (frames_any.at[:, 3 * core], outer_ref),
            (frames_any.at[2:4], late_ref),
        ],
        sems,
    )


def rim_kernel(own_ref, inner_ref, outer_ref, code_any, x_ref, rim_ref):
    core = lax.axis_index("c")
    for t in range(4):
        x_ref[t, 5 - 5 * core] = inner_ref[t]
        x_ref[t, 5 * core] = outer_ref[t]
    for t in range(2):
        rim_ref[t, 1 - core] = inner_ref[t + 2]
        rim_ref[t, core] = outer_ref[t + 2]


def early_kernel(earlier_ref, rim_ref, x_ref, early_ref):
    first = (lax.axis_index("z") == 0) & (lax.axis_index("x") == 0)

    @pl.when(first)
    def _():
        for t in range(2):
            early_ref[t] = x_ref[0]

    @pl.when(jnp.logical_not(first))
    def _():
        for t in range(2):
            early_ref[t, 0] = rim_ref[t, 0]
            early_ref[t, 5] = rim_ref[t, 1]
            for h in range(4):
                early_ref[t, h + 1] = earlier_ref[t, h]


def block_of(early_ref, x_ref):
    return lambda t, h: early_ref[t, h] if t < 2 else x_ref[t - 2, h]


def shifted_rows(value, step):
    row = lax.broadcasted_iota(jnp.int32, value.shape, 0)
    rolled = pltpu.roll(value, step % value.shape[0], 0)
    edge = 0 if step == 1 else value.shape[0] - 1
    return jnp.where(row == edge, 0.0, rolled)


def shifted_lanes(value, step):
    lane = lax.broadcasted_iota(jnp.int32, value.shape, 1)
    rolled = pltpu.roll(value, step % value.shape[1], 1)
    edge = 0 if step == 1 else value.shape[1] - 1
    return jnp.where(lane == edge, 0.0, rolled)


def forward_kernel(
    levels_ref,
    centres_ref,
    early_ref,
    x_ref,
    weight_ref,
    bias_ref,
    projection_ref,
    state_ref,
    quantized_ref,
    wide_out_ref,
):
    rows, columns, groups = centres_ref.shape
    channel = lax.broadcasted_iota(jnp.int32, (columns, groups), 0) % L
    half = half_ranges(levels_ref, channel)
    for h in range(rows):
        quantized_ref[h] = (centres_ref[h].astype(f32) - half) / half

    block = block_of(early_ref, x_ref)

    wide = jnp.concatenate(
        [jnp.concatenate([weight_ref[tap, c] for c in range(3)], 1) for tap in range(9)], 0
    )
    bias = bias_ref[...]
    pooled = [jnp.zeros((W, CH), f32) for _ in range(4)]
    for t in range(4):
        left = jnp.concatenate(
            [
                jnp.concatenate([block(t + a, h + b) for a in range(3) for b in range(3)], 1)
                for h in range(4)
            ],
            0,
        )
        wide_out_ref[...] = jnp.dot(left, wide, preferred_element_type=f32)
        for h in range(4):
            rows_h = slice(h * W, (h + 1) * W)
            preact = (
                bias
                + shifted_rows(wide_out_ref[rows_h, :CH], 1)
                + wide_out_ref[rows_h, CH : 2 * CH]
                + shifted_rows(wide_out_ref[rows_h, 2 * CH :], -1)
            )
            sigmoid = 0.5 * jnp.tanh(0.5 * preact) + 0.5
            place = (t * 4 + h) * W
            state_ref[place : place + W] = sigmoid * (1.0 + preact * (1.0 - sigmoid))
            pooled[h] = pooled[h] + (preact * sigmoid).astype(bf16).astype(f32)
    pooled = jnp.concatenate(pooled, 0) * 0.25
    state_ref[STATE : STATE + 4 * W] = pooled
    projection = jnp.concatenate([projection_ref[...], jnp.zeros((8 - L, CH), f32)], 0)
    latent = lax.dot_general(
        projection, pooled, (((1,), (1,)), ((), ())), precision=highest, preferred_element_type=f32
    )
    squashed = jnp.tanh(latent)
    for h in range(4):
        state_ref[SMALL + 8 * h : SMALL + 8 * h + 8] = squashed[:, h * W : (h + 1) * W]
    state_ref[SMALL + 32 : SMALL + 40] = projection
    channel = lax.broadcasted_iota(jnp.int32, (8, CH), 0)
    state_ref[SMALL + 40 : SMALL + 48] = half_ranges(levels_ref, channel)


def window(early_ref, x_ref, a, b):
    blocks = []
    if a < 2:
        blocks.append(early_ref[a:2, b : b + 4].reshape((2 - a) * 4 * W, CH))
    if a > 0:
        blocks.append(x_ref[max(a - 2, 0) : a + 2, b : b + 4].reshape(-1, CH))
    else:
        blocks.append(x_ref[0:2, b : b + 4].reshape(8 * W, CH))
    return jnp.concatenate(blocks, 0) if len(blocks) > 1 else blocks[0]


def backward_kernel(
    total_cells,
    early_ref,
    x_ref,
    state_ref,
    code_ref,
    theirs_ref,
    low_ref,
    small_ref,
):
    core = lax.axis_index("c")
    pooled = state_ref[STATE : STATE + 4 * W]
    squashed = jnp.concatenate(
        [state_ref[SMALL + 8 * h : SMALL + 8 * h + 8] for h in range(4)], 1
    )
    projection = state_ref[SMALL + 32 : SMALL + 40]
    half = state_ref[SMALL + 40 : SMALL + 48]
    tile_of = lax.broadcasted_iota(jnp.int32, (W, 32), 1)
    column = lax.broadcasted_iota(jnp.int32, (W, 32), 0)
    spread = jnp.where(column // 4 == tile_of, 1.0, 0.0).astype(f32)
    repeated = jnp.dot(spread, code_ref[...], precision=highest, preferred_element_type=f32)
    place = lax.broadcasted_iota(jnp.int32, (W, CH), 1)
    column = lax.broadcasted_iota(jnp.int32, (W, CH), 0)
    repeated = jnp.where((place % 24) // L == column % 4, repeated, 0.0)
    wanted = lax.broadcasted_iota(jnp.int32, (32, CH), 0)
    place = lax.broadcasted_iota(jnp.int32, (32, CH), 1)
    pick = jnp.where((place // 24 == wanted // 8) & (place % L == wanted % 8), 1.0, 0.0).astype(f32)
    codes = lax.dot_general(
        pick, repeated, (((1,), (1,)), ((), ())), precision=highest, preferred_element_type=f32
    )
    codes = jnp.concatenate([codes[8 * h : 8 * h + 8] / half for h in range(4)], 1)
    code_step = (
        (codes + 2.0 * commit_weight * offset_scale * squashed)
        * offset_scale
        * (1.0 - squashed * squashed)
        * float(total_cells) ** (-0.5)
    )
    projection_part = jnp.dot(code_step, pooled, precision=highest, preferred_element_type=f32)
    pooled_grad = 0.25 * lax.dot_general(
        code_step, projection, (((0,), (0,)), ((), ())), precision=highest, preferred_element_type=f32
    )
    bias_part = jnp.zeros((8, CH), f32)
    for t in range(4):
        for h in range(4):
            place = (t * 4 + h) * W
            pre_grad = pooled_grad[h * W : (h + 1) * W] * state_ref[place : place + W]
            bias_part = bias_part + pre_grad.reshape(W // 8, 8, CH).sum(0)
            turned = pre_grad.T
            low_ref[0:CH, place : place + W] = shifted_lanes(turned, -1).astype(bf16)
            low_ref[CH : 2 * CH, place : place + W] = turned.astype(bf16)
            low_ref[2 * CH :, place : place + W] = shifted_lanes(turned, 1).astype(bf16)
    bias_row = bias_part.sum(0, keepdims=True)
    row = lax.broadcasted_iota(jnp.int32, (8, CH), 0)
    small = jnp.where(row == L, bias_row, projection_part)
    pieces = split_small(small)
    small_ref[...] = pieces[0:8].astype(f32) + pieces[8:16].astype(f32)
    kernel_gradient(1 - core, early_ref, x_ref, low_ref, theirs_ref)
    for y in range(4):
        theirs_ref[y, :, LANES:] = pieces


def split_small(small):
    high = small.astype(bf16).astype(f32)
    return jnp.concatenate([high, small - high], 0).astype(bf16)


def kernel_gradient(core, early_ref, x_ref, low_ref, out_ref):
    starts = [pl.multiple_of(c * CH + 32 * y + 16 * core, 16) for c in range(3) for y in range(4)]
    left = jnp.concatenate([low_ref[pl.ds(start, 16), :] for start in starts], 0)
    taps = [(a, b) for a in range(3) for b in range(3)]
    for start in range(0, 9, 2):
        group = taps[start : start + 2]
        right = jnp.concatenate([window(early_ref, x_ref, a, b) for a, b in group], 1)
        result = jnp.dot(left, right, preferred_element_type=f32)
        for place in range(len(group)):
            for c in range(3):
                to = slice((3 * (start + place) + c) * CH, (3 * (start + place) + c + 1) * CH)
                for y in range(4):
                    row = (c * 4 + y) * 16
                    part = result[row : row + 16, place * CH : (place + 1) * CH]
                    out_ref[y, :, to] = part.astype(out_ref.dtype)


def own_kernel(early_ref, x_ref, low_ref, small_ref, mine_ref):
    kernel_gradient(lax.axis_index("c"), early_ref, x_ref, low_ref, mine_ref)
    for y in range(4):
        mine_ref[y, 0:8, LANES:] = small_ref[...]
        mine_ref[y, 8:16, LANES:] = jnp.zeros((8, CH), f32)


def pair_kernel(mine_ref, got_ref, out_ref):
    got_small = got_ref[0, :, LANES:].astype(f32)
    small = split_small(mine_ref[0, 0:8, LANES:] + (got_small[0:8] + got_small[8:16]))
    share = LANES // 32
    for y in range(4):
        total = mine_ref[y, :, :LANES] + got_ref[y, :, :LANES].astype(f32)
        for x in range(4):
            pieces = [
                total[:, (4 * z + x) * share : (4 * z + x + 1) * share] for z in range(8)
            ]
            dense = jnp.concatenate(pieces + [jnp.zeros((16, 7 * CH - 8 * share), f32)], 1)
            out_ref[x * 4 + y, :, : 7 * CH] = dense.astype(bf16)
            out_ref[x * 4 + y, :, 7 * CH :] = small


def plane_kernel(parts_ref, out_ref):
    total = parts_ref[0].astype(f32)
    for k in range(1, parts_ref.shape[0]):
        total = total + parts_ref[k].astype(f32)
    small = total[0:8, 7 * CH :] + total[8:16, 7 * CH :]
    share = LANES // 32
    for z in range(8):
        start = z * share
        base = start // CH * CH
        window = total[:, base : base + 2 * CH]
        if start > base:
            window = pltpu.roll(window, 2 * CH - (start - base), 1)
        out_ref[z, 0:16] = window[:, :CH]
        out_ref[z, 16:24] = small


def final_kernel(parts_ref, weight_ref, projection_ref, bias_ref):
    total = parts_ref[0]
    for k in range(1, parts_ref.shape[0]):
        total = total + parts_ref[k]
    weight_ref[...] = total[0:16, : weight_ref.shape[1]]
    projection_ref[...] = total[16 : 16 + L]
    bias_ref[...] = total[16 + L : 17 + L]


def on_device(frames, conv_weight, conv_bias, projection, levels, centres, code_grad):
    time_axes, row_axes, all_axes = ("z", "x"), ("y", "c"), ("z", "x", "y", "c")
    shards = 32
    strips = 8
    shape = jax.ShapeDtypeStruct
    dma = pltpu.SemaphoreType.DMA

    code_grad = jnp.transpose(code_grad, (1, 2, 0))
    centres = jnp.transpose(centres, (1, 2, 0))
    crossing = [(i, i + 1) for i in range(1, strips - 1, 2)]
    crossing = crossing + [(b, a) for a, b in crossing]
    edge = shape((4, W, CH), bf16)
    own = shape((4, 6, W, CH), bf16)
    later = [(i, i + 1) for i in range(shards - 1)]
    x, inner, outer, late = call(
        edge_kernel, [own, edge, edge, shape((2, 4, W, CH), bf16)], [ANY], [dma((4,))]
    )(frames)
    earlier = lax.ppermute(late, time_axes, later)
    outer = lax.ppermute(outer, row_axes, crossing)
    inner = lax.ppermute(inner, "c", [(0, 1), (1, 0)])
    (codes,) = call(code_kernel, [shape((shards, CH), f32)], [VMEM])(code_grad)
    x, rim = call(
        rim_kernel, [own, shape((2, 2, W, CH), bf16)], [VMEM] * 3 + [ANY], aliases={0: 0}
    )(x, inner, outer, codes)
    rim = lax.ppermute(rim, time_axes, later)
    codes = lax.all_to_all(codes.reshape(shards, 1, CH), time_axes, 0, 0, tiled=True)
    codes = codes.reshape(shards, CH)
    (early,) = call(early_kernel, [shape((2, 6, W, CH), bf16)], [VMEM] * 3)(earlier, rim, x)
    state, quantized = call(
        forward_kernel,
        [shape((SMALL + 48, CH), f32), shape(centres.shape, f32)],
        [VMEM] * 7,
        [pltpu.VMEM((4 * W, 3 * CH), f32)],
    )(
        levels.reshape(1, L),
        centres,
        early,
        x,
        conv_weight.reshape(9, 3, CH, CH),
        conv_bias.reshape(1, CH),
        projection.T,
    )

    total_cells = 4 * shards * 4 * strips * W
    theirs, low, small = call(
        lambda *refs: backward_kernel(total_cells, *refs),
        [shape((4, 16, WIDE), bf16), shape((3 * CH, 16 * W), bf16), shape((8, CH), f32)],
        [VMEM] * 4,
    )(early, x, state, codes)

    got = lax.ppermute(theirs, "c", [(0, 1), (1, 0)])
    (mine,) = call(own_kernel, [shape((4, 16, WIDE), f32)], [VMEM] * 4)(early, x, low, small)
    (chunks,) = call(pair_kernel, [shape((16, 16, 8 * CH), bf16)], [VMEM] * 2)(mine, got)
    chunks = lax.all_to_all(chunks, ("x", "y"), 0, 0, tiled=True)
    (chunks,) = call(plane_kernel, [shape((8, 24, CH), f32)], [VMEM])(chunks)
    parts = lax.all_to_all(chunks, "z", 0, 0, tiled=True)
    weight_grad, projection_grad, bias_grad = call(
        final_kernel,
        [shape((16, LANES // shards), f32), shape((L, CH), f32), shape((1, CH), f32)],
        [VMEM],
    )(parts)
    quantized = jnp.transpose(quantized, (2, 0, 1))
    return quantized, weight_grad.T, projection_grad.T, bias_grad.reshape(CH)


def solution(mesh):
    mesh = jax.sharding.Mesh(mesh.devices.reshape(8, 4, 4, 2), ("z", "x", "y", "c"))
    time, rows = ("z", "x"), ("y", "c")
    return jax.shard_map(
        on_device,
        mesh=mesh,
        in_specs=(
            P(time, rows, None, None),
            P(),
            P(),
            P(),
            P(),
            P(None, rows, time),
            P(None, rows, time),
        ),
        out_specs=(P(None, rows, time), P(time, rows), P(), P()),
        check_vma=False,
    )
```
